32 devices in a mesh: dp: 16 (over z, y, core), mp: 2 (over x).
Axes of the slice: x: 2, y: 2, z: 4, core: 2. Of those that a mesh axis runs over, the one named last changes fastest.
Arguments:
- frames_in: bfloat16 [16384, 1536], P('dp', 'mp')
- lengths: int32 [64], P('dp'), may hold values from 42 to 256, as said below
- ln_gain: float32 [1536], P('mp'), may hold values from 0.1 to 1.9
- ln_bias: float32 [1536], P('mp'), may hold values from -3 to 3
- kernel: float32 [31, 1536], P(None, 'mp'), may hold values from -1 to 1
- point_weight: bfloat16 [1536, 1536], P('dp', 'mp'), may hold values from -0.15625 to 0.15625
- target: bfloat16 [16384, 1536], P('dp')
Outputs:
- frames_grad: bfloat16 [16384, 1536], P('dp', 'mp')
- weight_grad: float32 [1536, 1536], P('dp', 'mp')
- kernel_grad: float32 [31, 1536], P(None, 'mp')
- gain_grad: float32 [1536], P('mp')
- bias_grad: float32 [1536], P('mp')
The draws below stay inside these ranges and needn't reach their ends.
Inputs may be any that keep to these rules, and one draw needn't show every extreme that they name: `lengths`: valid frames of each utterance slot; some slot has exactly 256.
All inputs are finite; a program needn't handle non-finite values.
Results may differ from the reference program's by a relative error of at most 0.001.
Values may be sent and summed in bfloat16 or wider, within the bound.
A program may use at most 64 MiB of HBM per device.

```python
import math
import jax
import jax.numpy as jnp
from jax import lax

D = 1536
KERNEL = 31
UTT = 4
FRAMES = 256
TOK_DEV = 1024
TOKENS = 16384
UTTS = 64
N_DP = 16


def draw_lengths(key, part):
    slot_index = jnp.arange(UTTS, dtype=jnp.int32)
    device_index = slot_index // UTT
    floor_top = FRAMES // 3
    ceiling = floor_top + device_index * (FRAMES - floor_top) // max(N_DP - 1, 1)
    low_end = ceiling // 2
    random_bits = jax.random.randint(key, (UTTS,), 0, 1 << 20)
    drawn = low_end + random_bits % (ceiling - low_end + 1)
    drawn = jnp.where(slot_index == UTTS - 1, FRAMES, drawn)
    drawn = jnp.where(slot_index == 0, floor_top // 2, drawn)
    return drawn.astype(jnp.int32)


def draw_frames_in(key, part):
    first, second, third, fourth = jax.random.split(jax.random.fold_in(key, 11), 4)
    ramp = jnp.arange(D, dtype=jnp.float32) / max(D - 1, 1)
    col_scale = jnp.exp(jax.random.uniform(first, (D,), jnp.float32, 0.0, math.log(10.0)) + math.log(3.0) * ramp)
    offset = 0.8 * jax.random.normal(second, (D,), jnp.float32)
    row_scale = jnp.exp(jax.random.uniform(fourth, (TOKENS, 1), jnp.float32, 0.0, math.log(10.0)))
    noise = jax.random.normal(third, (TOKENS, D), jnp.float32)
    return ((offset + noise) * col_scale * row_scale).astype(jnp.bfloat16)


def draw_target(key, part):
    first, second = jax.random.split(jax.random.fold_in(key, 23), 2)
    common = jax.random.normal(first, (D,), jnp.float32)
    noise = jax.random.normal(second, (TOKENS, D), jnp.float32)
    return jnp.clip(common + noise, -6.0, 6.0).astype(jnp.bfloat16)


def level_of(stream_key, dims, shards, smallest, high):
    factor_of, own = 1.0, jax.random.fold_in(stream_key, 6)
    for axis_at, parts in shards:
        draws = jnp.exp(jax.random.uniform(jax.random.fold_in(own, axis_at), (parts,), jnp.float32, smallest / len(shards), high / len(shards)))
        factor_of = factor_of * jnp.repeat(draws, dims[axis_at] // parts).reshape([-1 if axis == axis_at else 1 for axis in range(len(dims))])
    return factor_of


def scatter_about(own_key, dims, scale, reach, shards=(), held_as=jnp.bfloat16):
    values = scale * jax.random.normal(own_key, dims, jnp.float32)
    if shards:
        values = values * level_of(own_key, dims, shards, -0.22, 0.18)
    return jnp.clip(values, -reach, reach).astype(held_as)


def setup_inputs(seed: int = 0) -> dict:
    key_of = jax.random.split(jax.random.key(seed), 8)
    frames_in = draw_frames_in(jax.random.fold_in(key_of[7], 71), 0)
    lengths = draw_lengths(jax.random.fold_in(key_of[7], 71), 0)
    ln_gain = jnp.clip(1.0 + 0.18 * jax.random.normal(key_of[2], (D,), jnp.float32), 0.1, 1.9)
    ln_bias = scatter_about(key_of[3], (D,), 0.5, 3.0, ((0, 2),), jnp.float32)
    kernel = scatter_about(key_of[4], (KERNEL, D), KERNEL ** -0.5, 1.0, ((1, 2),), jnp.float32)
    point_weight = scatter_about(key_of[5], (D, D), D ** -0.5, 0.15625, ((0, 16), (1, 2)))
    target = draw_target(jax.random.fold_in(key_of[7], 71), 0)
    return dict(frames_in=frames_in, lengths=lengths, ln_gain=ln_gain, ln_bias=ln_bias, kernel=kernel, point_weight=point_weight, target=target)


epsilon = 1e-05

def reference(frames_in, lengths, ln_gain, ln_bias, kernel, point_weight, target):
    frame_total = jnp.sum(lengths).astype(jnp.float32)
    inverse = 1.0 / frame_total
    half = (KERNEL - 1) // 2

    def block(state_carry, block_inputs):
        grad_acc, kernel_acc, gain_acc, bias_acc = state_carry
        x_block, len_block, target_block = block_inputs
        position = lax.broadcasted_iota(jnp.int32, (UTT, FRAMES), 1)
        valid_mask = (position < len_block[:, None]).astype(jnp.float32).reshape(TOK_DEV, 1)
        values = x_block.astype(jnp.float32)
        row_mean = lax.optimization_barrier(jnp.mean(values, axis=1, keepdims=True))
        centered = values - row_mean
        row_var = lax.optimization_barrier(jnp.mean(centered * centered, axis=1, keepdims=True))
        inv_std = lax.rsqrt(row_var + epsilon)
        normed = centered * inv_std
        masked = (normed * ln_gain + ln_bias) * valid_mask
        padded = jnp.pad(masked.reshape(UTT, FRAMES, D), ((0, 0), (half, half), (0, 0)))
        conv_out = jnp.zeros((UTT, FRAMES, D), jnp.float32)
        for k in range(KERNEL):
            conv_out = conv_out + kernel[k] * padded[:, k:k + FRAMES, :]
        pre_act = conv_out.reshape(TOK_DEV, D)
        gate_sig = jax.nn.sigmoid(pre_act)
        activation = (pre_act * gate_sig).astype(jnp.bfloat16)
        cotangent = target_block * valid_mask.astype(jnp.bfloat16)
        grad_acc = grad_acc + lax.dot_general(cotangent, activation, (((0,), (0,)), ((), ())), preferred_element_type=jnp.float32)
        act_grad = jnp.dot(cotangent, point_weight, preferred_element_type=jnp.float32)
        pre_grad = act_grad * gate_sig * (1.0 + pre_act * (1.0 - gate_sig))
        grad_block = pre_grad.reshape(UTT, FRAMES, D)
        grad_padded = jnp.pad(grad_block, ((0, 0), (half, half), (0, 0)))
        back_in = jnp.zeros((UTT, FRAMES, D), jnp.float32)
        kernel_rows = []
        for k in range(KERNEL):
            back_in = back_in + kernel[k] * grad_padded[:, 2 * half - k:2 * half - k + FRAMES, :]
            kernel_rows.append(lax.optimization_barrier(jnp.sum(grad_block * padded[:, k:k + FRAMES, :], axis=(0, 1))))
        kernel_part = jnp.stack(kernel_rows, axis=0)
        masked_grad = back_in.reshape(TOK_DEV, D) * valid_mask
        gain_acc = gain_acc + lax.optimization_barrier(jnp.sum(masked_grad * normed, axis=0))
        bias_acc = bias_acc + lax.optimization_barrier(jnp.sum(masked_grad, axis=0))
        kernel_acc = kernel_acc + kernel_part
        hat_grad = masked_grad * ln_gain
        norm_grad = inv_std * (hat_grad - lax.optimization_barrier(jnp.mean(hat_grad, axis=1, keepdims=True)) - normed * lax.optimization_barrier(jnp.mean(hat_grad * normed, axis=1, keepdims=True)))
        frames_out = ((cotangent.astype(jnp.float32) + norm_grad) * (TOKENS * inverse)).astype(jnp.bfloat16)
        return ((grad_acc, kernel_acc, gain_acc, bias_acc), frames_out)
    start_state = (jnp.zeros((D, D), jnp.float32), jnp.zeros((KERNEL, D), jnp.float32), jnp.zeros((D,), jnp.float32), jnp.zeros((D,), jnp.float32))
    final_state, frames_blocks = lax.scan(block, start_state, (frames_in.reshape(N_DP, TOK_DEV, D), lengths.reshape(N_DP, UTT), target.reshape(N_DP, TOK_DEV, D)))
    grad_acc, kernel_acc, gain_acc, bias_acc = final_state
    return (frames_blocks.reshape(TOKENS, D), grad_acc * inverse, kernel_acc * inverse, gain_acc * inverse, bias_acc * inverse)
```

```python
import functools

import jax
import jax.numpy as jnp
from jax import lax
from jax.experimental import pallas as pl
from jax.experimental.pallas import tpu as pltpu
from jax.sharding import PartitionSpec as P

epsilon = 1e-05
LANES = 128
CHUNK = 64
F32 = jnp.float32
BF16 = jnp.bfloat16


def depthwise(inputs, taps):
    half = (taps.shape[0] - 1) // 2
    return lax.conv_general_dilated(
        inputs,
        taps[:, None, :],
        (1,),
        [(half, half)],
        dimension_numbers=("NWC", "WIO", "NWC"),
        feature_group_count=inputs.shape[2],
        precision=lax.Precision.HIGHEST,
    )


def plain_body(frames_in, lengths, ln_gain, ln_bias, kernel, point_weight, target):
    tok_rows, chan_count = frames_in.shape
    utt_count = lengths.shape[0]
    frame_count = tok_rows // utt_count
    full_width = target.shape[1]
    position = lax.broadcasted_iota(jnp.int32, (utt_count, frame_count), 1)
    valid_mask = (position < lengths[:, None]).astype(jnp.float32).reshape(tok_rows, 1)
    local_total = jnp.sum(lengths).astype(jnp.float32)
    values = frames_in.astype(jnp.float32)
    row_mean = lax.psum(jnp.sum(values, axis=1), "mp") / full_width
    centered = values - row_mean[:, None]
    row_var = lax.psum(jnp.sum(centered * centered, axis=1), "mp") / full_width
    inv_std = lax.rsqrt(row_var + epsilon)[:, None]
    normed = centered * inv_std
    masked = (normed * ln_gain + ln_bias) * valid_mask
    conv_out, conv_back = jax.vjp(
        depthwise, masked.reshape(utt_count, frame_count, chan_count), kernel
    )
    pre_act = conv_out.reshape(tok_rows, chan_count)
    gate_sig = jax.nn.sigmoid(pre_act)
    activation = (pre_act * gate_sig).astype(jnp.bfloat16)
    cotangent = target * valid_mask.astype(jnp.bfloat16)
    act_grad = jnp.dot(
        cotangent,
        lax.all_gather(point_weight, "dp", axis=0, tiled=True),
        preferred_element_type=jnp.float32,
    )
    pre_grad = act_grad * gate_sig * (1.0 + pre_act * (1.0 - gate_sig))
    back_in, kernel_part = conv_back(pre_grad.reshape(utt_count, frame_count, chan_count))
    masked_grad = back_in.reshape(tok_rows, chan_count) * valid_mask
    gain_part = jnp.sum(masked_grad * normed, axis=0)
    bias_part = jnp.sum(masked_grad, axis=0)
    hat_grad = masked_grad * ln_gain
    hat_sum, hat_dot = lax.psum(
        (jnp.sum(hat_grad, axis=1), jnp.sum(hat_grad * normed, axis=1)), "mp"
    )
    norm_grad = inv_std * (
        hat_grad - hat_sum[:, None] / full_width - normed * (hat_dot[:, None] / full_width)
    )
    term = lax.dot_general(
        cotangent, activation, (((0,), (0,)), ((), ())), preferred_element_type=jnp.float32
    )
    weight_grad = lax.psum_scatter(term, "dp", scatter_dimension=0, tiled=True)
    kernel_sum, gain_sum, bias_sum, frame_total = lax.psum(
        (kernel_part, gain_part, bias_part, local_total), "dp"
    )
    inverse = 1.0 / frame_total
    own_grad = lax.dynamic_slice_in_dim(
        cotangent, lax.axis_index("mp") * chan_count, chan_count, 1
    ).astype(jnp.float32)
    slot_total = tok_rows * lax.axis_size("dp")
    frames_grad = ((own_grad + norm_grad) * (slot_total * inverse)).astype(jnp.bfloat16)
    return (
        frames_grad,
        weight_grad * inverse,
        kernel_sum * inverse,
        gain_sum * inverse,
        bias_sum * inverse,
    )


def rcopy(src, dst, sends, recvs, at, peer):
    return pltpu.make_async_remote_copy(
        src_ref=src,
        dst_ref=dst,
        send_sem=sends.at[at],
        recv_sem=recvs.at[at],
        device_id=peer,
        device_id_type=pl.DeviceIdType.MESH,
    )


def mp_peers(mp):
    me_dp, me_mp = lax.axis_index("dp"), lax.axis_index("mp")
    return [(me_dp, lax.rem(me_mp + s, mp)) for s in range(1, mp)]


def dp_bits(stages):
    me_dp, me_mp = lax.axis_index("dp"), lax.axis_index("mp")
    bits = [(me_dp // (1 << s)) % 2 for s in range(stages)]
    peers = [(me_dp + (1 << s) * (1 - 2 * bits[s]), me_mp) for s in range(stages)]
    return bits, peers


def greet(peers):
    barrier = pltpu.get_barrier_semaphore()
    for peer in peers:
        pl.semaphore_signal(
            barrier, inc=1, device_id=peer, device_id_type=pl.DeviceIdType.MESH
        )
    pl.semaphore_wait(barrier, len(peers))


def eye_mask():
    shape = (LANES, LANES)
    return lax.broadcasted_iota(jnp.int32, shape, 0) == lax.broadcasted_iota(jnp.int32, shape, 1)


def to_row(column, eye):
    return jnp.sum(jnp.where(eye, column, 0.0), axis=0, keepdims=True)


def to_column(row, eye):
    return jnp.sum(jnp.where(eye, row, 0.0), axis=1, keepdims=True)


def lane_at(c):
    return pl.ds(pl.multiple_of(c * LANES, LANES), LANES)


def rows_at(start, size, unit):
    return pl.ds(pl.multiple_of(start, unit), size)


def valid_rows(len_ref, u, start, size):
    position = start + lax.broadcasted_iota(jnp.int32, (size, LANES), 0)
    return position < len_ref[u]


def forward_kernel(
    mp, utts, frames, taps, pad,
    len_ref, x_ref, gain_ref, bias_ref, tap_ref, target_ref,
    masked_ref, pre_ref, act_ref, cot_ref, mean_ref, rstd_ref,
    stat, got, sends, recvs,
):
    tok, chan = x_ref.shape
    groups = tok // LANES
    blocks = chan // LANES
    span = frames + 2 * pad
    peers = mp_peers(mp)
    greet(peers)
    eye = eye_mask()

    def stats(g, _):
        values = x_ref[rows_at(g * LANES, LANES, LANES), :].astype(F32)
        local = jnp.sum(values, axis=1, keepdims=True) * (1.0 / chan)
        off = values - local
        squares = jnp.sum(off * off, axis=1, keepdims=True)
        stat[0, pl.ds(g, 1), :] = to_row(local, eye)
        stat[1, pl.ds(g, 1), :] = to_row(squares, eye)
        return 0

    lax.fori_loop(0, groups, stats, 0)
    copies = [
        rcopy(stat, got.at[s], sends, recvs, s, peer) for s, peer in enumerate(peers)
    ]
    for copy in copies:
        copy.start()

    def mask_target(i, _):
        u, part = i // (frames // CHUNK), i % (frames // CHUNK)
        rows = rows_at(i * CHUNK, CHUNK, CHUNK)
        valid = valid_rows(len_ref, u, part * CHUNK, CHUNK)
        for c in range(target_ref.shape[1] // LANES):
            lanes = pl.ds(c * LANES, LANES)
            block = target_ref[rows, lanes].astype(F32)
            cot_ref[rows, lanes] = jnp.where(valid, block, 0.0).astype(BF16)
        return 0

    lax.fori_loop(0, tok // CHUNK, mask_target, 0)

    def clear(i, _):
        c, u = i // utts, i % utts
        edge = jnp.zeros((pad, LANES), F32)
        masked_ref[c, rows_at(u * span, pad, pad), :] = edge
        masked_ref[c, rows_at(u * span + pad + frames, pad, pad), :] = edge
        return 0

    lax.fori_loop(0, blocks * utts, clear, 0)
    for copy in copies:
        copy.wait()
    mean = stat[0]
    for s in range(mp - 1):
        mean = mean + got[s, 0]
    mean = mean * (1.0 / mp)
    squares = stat[1] + chan * (stat[0] - mean) * (stat[0] - mean)
    for s in range(mp - 1):
        squares = squares + (got[s, 1] + chan * (got[s, 0] - mean) * (got[s, 0] - mean))
    stat[0] = mean
    stat[1] = lax.rsqrt(squares * (1.0 / (chan * mp)) + epsilon)

    def spread(g, _):
        rows = rows_at(g * LANES, LANES, LANES)
        shape = (LANES, LANES)
        mean_ref[rows, :] = jnp.broadcast_to(to_column(stat[0, pl.ds(g, 1), :], eye), shape)
        rstd_ref[rows, :] = jnp.broadcast_to(to_column(stat[1, pl.ds(g, 1), :], eye), shape)
        return 0

    lax.fori_loop(0, groups, spread, 0)

    def block(c, _):
        lanes = lane_at(c)
        gain, bias = gain_ref[c], bias_ref[c]

        def norm(i, _):
            u, part = i // (frames // CHUNK), i % (frames // CHUNK)
            rows = rows_at(i * CHUNK, CHUNK, CHUNK)
            values = x_ref[rows, lanes].astype(F32)
            normed = (values - mean_ref[rows, :]) * rstd_ref[rows, :]
            valid = valid_rows(len_ref, u, part * CHUNK, CHUNK)
            masked_ref[c, rows_at(u * span + pad + part * CHUNK, CHUNK, 16), :] = jnp.where(
                valid, normed * gain + bias, 0.0
            )
            return 0

        lax.fori_loop(0, tok // CHUNK, norm, 0)

        def conv(i, _):
            u, part = i // (frames // CHUNK), i % (frames // CHUNK)
            rows = rows_at(i * CHUNK, CHUNK, CHUNK)
            base = u * span + part * CHUNK
            shift = pad - (taps - 1) // 2
            total = jnp.zeros((CHUNK, LANES), F32)
            for b in range(8):
                ks = [k for k in range(taps) if (k + shift) % 8 == b]
                reach = 8 * max((k + shift) // 8 for k in ks)
                slab = masked_ref[c, pl.ds(base + b, CHUNK + reach), :]
                for k in ks:
                    at = (k + shift) // 8 * 8
                    total = total + tap_ref[c, pl.ds(k, 1), :] * slab[at:at + CHUNK]
            pre_ref[c, rows, :] = total
            act_ref[rows, lanes] = (total * jax.nn.sigmoid(total)).astype(BF16)
            return 0

        lax.fori_loop(0, tok // CHUNK, conv, 0)
        return 0

    lax.fori_loop(0, blocks, block, 0)


def backward_kernel(
    mp, stages, utts, frames, taps, pad,
    len_ref, x_ref, gain_ref, tap_ref, weight_ref,
    masked_ref, pre_ref, act_ref, cot_ref, mean_ref, rstd_ref,
    out_ref, wgrad_ref, small_ref,
    term, core_got, a1, a2, a3, b1, b2, b3,
    pgrad, hat, hat_sum, hat_dot, tap_acc, stat, got, count, count_got, small, small_got,
    core_s, core_r, ring_s, ring_r, hat_s, hat_r, cnt_s, cnt_r, sm_s, sm_r,
):
    tok, chan = x_ref.shape
    width = cot_ref.shape[1]
    groups = tok // LANES
    blocks = chan // LANES
    span = frames + 2 * pad
    per_utt = frames // CHUNK
    half = chan // 2
    out_rows = wgrad_ref.shape[0]
    highs = term.shape[0]
    row_peers = mp_peers(mp)
    bits, peers = dp_bits(stages)
    greet(peers + row_peers)
    core, why, zlo, zhi = bits
    eye = eye_mask()

    total = len_ref[0]
    for u in range(1, utts):
        total = total + len_ref[u]
    count[0] = jnp.full((8, LANES), total, jnp.int32).astype(F32)
    cnt = [
        rcopy(count.at[s], count_got.at[s], cnt_s, cnt_r, s, peers[s]) for s in range(stages)
    ]
    cnt[0].start()
    core_copies = []
    group_rows = width // highs
    for g in range(highs):
        product = lax.dot_general(
            cot_ref[:, g * group_rows:(g + 1) * group_rows],
            act_ref[...],
            (((0,), (0,)), ((), ())),
            preferred_element_type=F32,
        )
        for y in range(2):
            for k in range(2):
                at = (2 * y + k) * out_rows
                term[g, y, k] = product[at:at + out_rows]
        copy = rcopy(
            term.at[g, :, 1 - core], core_got.at[g], core_s, core_r, g, peers[0]
        )
        copy.start()
        core_copies.append(copy)
        cnt[g].wait()
        count[g + 1] = count[g] + count_got[g]
        if g + 1 < stages:
            cnt[g + 1].start()
    inverse = 1.0 / count[stages]

    def clear(i, _):
        c, u = i // utts, i % utts
        edge = jnp.zeros((pad, LANES), F32)
        pgrad[c, rows_at(u * span, pad, pad), :] = edge
        pgrad[c, rows_at(u * span + pad + frames, pad, pad), :] = edge
        return 0

    lax.fori_loop(0, blocks * utts, clear, 0)

    def act_grad(u, _):
        rows = rows_at(u * frames, frames, frames)
        product = jnp.dot(cot_ref[rows, :], weight_ref[...], preferred_element_type=F32)
        for c in range(blocks):
            pre = pre_ref[c, rows, :]
            gate = jax.nn.sigmoid(pre)
            grad = product[:, c * LANES:(c + 1) * LANES]
            pgrad[c, rows_at(u * span + pad, frames, 16), :] = (
                grad * gate * (1.0 + pre * (1.0 - gate))
            )
        return 0

    lax.fori_loop(0, utts, act_grad, 0)

    for copy in core_copies:
        copy.wait()

    def join_core(i, _):
        g, y = i // 2, i % 2
        core_got[g, y] = core_got[g, y] + term[g, y, core]
        return 0

    lax.fori_loop(0, highs * 2, join_core, 0)
    left, right = pl.ds(0, half), pl.ds(half, half)

    copy_a1 = rcopy(core_got.at[:, 1 - why, :, left], a1, ring_s, ring_r, 0, peers[1])
    copies_b1 = [
        rcopy(
            core_got.at[2 * h + 1 - zlo, :, :, right], b1.at[h], ring_s, ring_r, 1 + h, peers[2]
        )
        for h in range(2)
    ]
    copies_a2 = [
        rcopy(a1.at[2 * h + 1 - zlo], a2.at[h], ring_s, ring_r, 3 + h, peers[2])
        for h in range(2)
    ]
    copy_b2 = rcopy(b1.at[1 - zhi], b2, ring_s, ring_r, 5, peers[3])
    copy_a3 = rcopy(a2.at[1 - zhi], a3, ring_s, ring_r, 6, peers[3])
    copy_b3 = rcopy(b2.at[1 - why], b3, ring_s, ring_r, 7, peers[1])

    copy_a1.start()
    for copy in copies_b1:
        copy.start()

    def second_stage():
        copy_a1.wait()
        for h in range(highs):
            a1[h] = a1[h] + core_got[h, why, :, left]
        for copy in copies_a2:
            copy.start()
        for copy in copies_b1:
            copy.wait()
        for h in range(2):
            for y in range(2):
                b1[h, y] = b1[h, y] + core_got[2 * h + zlo, y, :, right]
        copy_b2.start()

    def third_stage():
        for copy in copies_a2:
            copy.wait()
        for h in range(2):
            a2[h] = a2[h] + a1[2 * h + zlo]
        copy_a3.start()
        copy_b2.wait()
        for y in range(2):
            b2[y] = b2[y] + b1[zhi, y]
        copy_b3.start()

    def last_stage():
        scale = inverse[0:1, 0:1]
        copy_a3.wait()
        wgrad_ref[:, 0:half] = (a3[...] + a2[zhi]) * scale
        copy_b3.wait()
        wgrad_ref[:, half:chan] = (b3[...] + b2[why]) * scale

    shift = pad - (taps - 1) // 2

    def block(c, _):
        lanes = lane_at(c)
        gain = gain_ref[c]
        tap_acc[...] = jnp.zeros_like(tap_acc)

        def part_of(i, _):
            u, part = i // per_utt, i % per_utt
            rows = rows_at(i * CHUNK, CHUNK, CHUNK)
            base = u * span + part * CHUNK
            total = jnp.zeros((CHUNK, LANES), F32)
            grads = pgrad[c, rows_at(base + pad, CHUNK, 16), :]
            for b in range(8):
                ks = [k for k in range(taps) if (k + shift) % 8 == b]
                reach = 8 * max((k + shift) // 8 for k in ks)
                slab = pgrad[c, pl.ds(base + b, CHUNK + reach), :]
                for k in ks:
                    at = (k + shift) // 8 * 8
                    total = total + tap_ref[c, pl.ds(taps - 1 - k, 1), :] * slab[at:at + CHUNK]
            for b in range(8):
                ks = [k for k in range(taps) if (k + shift) % 8 == b]
                reach = 8 * max((k + shift) // 8 for k in ks)
                slab = masked_ref[c, pl.ds(base + b, CHUNK + reach), :]
                for k in ks:
                    at = (k + shift) // 8 * 8
                    part_sum = grads * slab[at:at + CHUNK]
                    tap_acc[k] += jnp.sum(part_sum.reshape(CHUNK // 8, 8, LANES), axis=0)
            valid = valid_rows(len_ref, u, part * CHUNK, CHUNK)
            masked_grad = jnp.where(valid, total, 0.0)
            normed = (x_ref[rows, lanes].astype(F32) - mean_ref[rows, :]) * rstd_ref[rows, :]
            scaled = masked_grad * normed
            tap_acc[taps] += jnp.sum(scaled.reshape(CHUNK // 8, 8, LANES), axis=0)
            tap_acc[taps + 1] += jnp.sum(masked_grad.reshape(CHUNK // 8, 8, LANES), axis=0)
            grad = masked_grad * gain
            hat[c, rows, :] = grad
            hat_sum[rows, :] += grad
            hat_dot[rows, :] += scaled * gain
            return 0

        lax.fori_loop(0, tok // CHUNK, part_of, 0)
        sums = jnp.sum(tap_acc[...], axis=1)
        small[0, :, lanes] = sums
        return 0

    def reset(i, _):
        rows = rows_at(i * CHUNK, CHUNK, CHUNK)
        hat_sum[rows, :] = jnp.zeros((CHUNK, LANES), F32)
        hat_dot[rows, :] = jnp.zeros((CHUNK, LANES), F32)
        return 0

    lax.fori_loop(0, tok // CHUNK, reset, 0)
    cut = [0, blocks // 2, blocks - blocks // 6, blocks]
    lax.fori_loop(cut[0], cut[1], block, 0)
    second_stage()
    lax.fori_loop(cut[1], cut[2], block, 0)
    third_stage()
    lax.fori_loop(cut[2], cut[3], block, 0)

    def collect(g, _):
        rows = rows_at(g * LANES, LANES, LANES)
        stat[0, pl.ds(g, 1), :] = to_row(jnp.sum(hat_sum[rows, :], axis=1, keepdims=True), eye)
        stat[1, pl.ds(g, 1), :] = to_row(jnp.sum(hat_dot[rows, :], axis=1, keepdims=True), eye)
        return 0

    sm = [
        rcopy(small.at[s], small_got.at[s], sm_s, sm_r, s, peers[s]) for s in range(stages)
    ]
    sm[0].start()
    lax.fori_loop(0, groups, collect, 0)
    hats = [
        rcopy(stat, got.at[s], hat_s, hat_r, s, peer) for s, peer in enumerate(row_peers)
    ]
    for copy in hats:
        copy.start()
    sm[0].wait()
    small[1] = small[0] + small_got[0]
    sm[1].start()
    for copy in hats:
        copy.wait()
    for j in range(2):
        joined = stat[j]
        for s in range(mp - 1):
            joined = joined + got[s, j]
        stat[j] = joined * (1.0 / width)

    def spread(g, _):
        rows = rows_at(g * LANES, LANES, LANES)
        shape = (LANES, LANES)
        hat_sum[rows, :] = jnp.broadcast_to(to_column(stat[0, pl.ds(g, 1), :], eye), shape)
        hat_dot[rows, :] = jnp.broadcast_to(to_column(stat[1, pl.ds(g, 1), :], eye), shape)
        return 0

    lax.fori_loop(0, groups, spread, 0)
    own = lax.axis_index("mp") * blocks
    slots = (tok * (1 << stages)) * inverse[0:1, :]

    def finish(i, _):
        rows = rows_at(i * CHUNK, CHUNK, CHUNK)
        mean, rstd = mean_ref[rows, :], rstd_ref[rows, :]
        sums, dots = hat_sum[rows, :], hat_dot[rows, :]
        for c in range(blocks):
            lanes = pl.ds(c * LANES, LANES)
            normed = (x_ref[rows, lanes].astype(F32) - mean) * rstd
            grad = rstd * (hat[c, rows, :] - sums - normed * dots)
            direct = cot_ref[rows, lane_at(own + c)].astype(F32)
            out_ref[rows, lanes] = ((direct + grad) * slots).astype(BF16)
        return 0

    parts = tok // CHUNK
    marks = [parts * s // (stages - 1) for s in range(stages)]
    for s in range(1, stages):
        lax.fori_loop(marks[s - 1], marks[s], finish, 0)
        sm[s].wait()
        small[s + 1] = small[s] + small_got[s]
        if s + 1 < stages:
            sm[s + 1].start()
    small_ref[...] = small[stages] * inverse[0:1, 0:1]
    last_stage()


def fast_body(dp, mp, frames_in, lengths, ln_gain, ln_bias, kernel, point_weight, target):
    tok, chan = frames_in.shape
    utts = lengths.shape[0]
    frames = tok // utts
    width = target.shape[1]
    taps = kernel.shape[0]
    pad = 16
    blocks = chan // LANES
    stages = dp.bit_length() - 1
    groups = tok // LANES
    span = utts * (frames + 2 * pad)
    out_rows = width // dp
    highs = dp // 4
    half = chan // 2
    gathered = lax.all_gather(point_weight, "dp", axis=0, tiled=True)
    gain = ln_gain.reshape(blocks, 1, LANES)
    bias = ln_bias.reshape(blocks, 1, LANES)
    tap_blocks = kernel.reshape(taps, blocks, LANES).transpose(1, 0, 2)
    vmem = pl.BlockSpec(memory_space=pltpu.VMEM)
    smem = pl.BlockSpec(memory_space=pltpu.SMEM)
    dma = pltpu.SemaphoreType.DMA
    shape = jax.ShapeDtypeStruct
    peers = max(mp - 1, 1)
    masked, pre, act, cot, mean, rstd = pl.pallas_call(
        functools.partial(forward_kernel, mp, utts, frames, taps, pad),
        out_shape=(
            shape((blocks, span, LANES), F32),
            shape((blocks, tok, LANES), F32),
            shape((tok, chan), BF16),
            shape((tok, width), BF16),
            shape((tok, LANES), F32),
            shape((tok, LANES), F32),
        ),
        in_specs=[smem] + [vmem] * 5,
        out_specs=(vmem,) * 6,
        scratch_shapes=[
            pltpu.VMEM((2, groups, LANES), F32),
            pltpu.VMEM((peers, 2, groups, LANES), F32),
            dma((peers,)),
            dma((peers,)),
        ],
        compiler_params=pltpu.CompilerParams(
            collective_id=0, has_side_effects=True, vmem_limit_bytes=40 * 2**20
        ),
        cost_estimate=pl.CostEstimate(
            flops=40 * tok * chan * taps, bytes_accessed=24 * tok * chan, transcendentals=tok * chan
        ),
        name="forward",
    )(lengths, frames_in, gain, bias, tap_blocks, target)
    side = (taps + 2 + 7) // 8 * 8
    frames_grad, weight_grad, small = pl.pallas_call(
        functools.partial(backward_kernel, mp, stages, utts, frames, taps, pad),
        out_shape=(
            shape((tok, chan), BF16),
            shape((out_rows, chan), F32),
            shape((side, chan), F32),
        ),
        in_specs=[smem] + [vmem] * 10,
        out_specs=(vmem,) * 3,
        scratch_shapes=[
            pltpu.VMEM((highs, 2, 2, out_rows, chan), F32),
            pltpu.VMEM((highs, 2, out_rows, chan), F32),
            pltpu.VMEM((highs, out_rows, half), F32),
            pltpu.VMEM((2, out_rows, half), F32),
            pltpu.VMEM((out_rows, half), F32),
            pltpu.VMEM((2, 2, out_rows, half), F32),
            pltpu.VMEM((2, out_rows, half), F32),
            pltpu.VMEM((out_rows, half), F32),
            pltpu.VMEM((blocks, span, LANES), F32),
            pltpu.VMEM((blocks, tok, LANES), F32),
            pltpu.VMEM((tok, LANES), F32),
            pltpu.VMEM((tok, LANES), F32),
            pltpu.VMEM((side, 8, LANES), F32),
            pltpu.VMEM((2, groups, LANES), F32),
            pltpu.VMEM((peers, 2, groups, LANES), F32),
            pltpu.VMEM((stages + 1, 8, LANES), F32),
            pltpu.VMEM((stages, 8, LANES), F32),
            pltpu.VMEM((stages + 1, side, chan), F32),
            pltpu.VMEM((stages, side, chan), F32),
            dma((highs,)),
            dma((highs,)),
            dma((8,)),
            dma((8,)),
            dma((peers,)),
            dma((peers,)),
            dma((stages,)),
            dma((stages,)),
            dma((stages,)),
            dma((stages,)),
        ],
        compiler_params=pltpu.CompilerParams(
            collective_id=1, has_side_effects=True, vmem_limit_bytes=56 * 2**20
        ),
        name="backward",
    )(lengths, frames_in, gain, tap_blocks, gathered, masked, pre, act, cot, mean, rstd)
    return (frames_grad, weight_grad, small[:taps], small[taps], small[taps + 1])


def solution(mesh):
    dp, mp = mesh.shape["dp"], mesh.shape["mp"]

    def body(frames_in, lengths, ln_gain, ln_bias, kernel, point_weight, target):
        args = (frames_in, lengths, ln_gain, ln_bias, kernel, point_weight, target)
        tok, chan = frames_in.shape
        frames = tok // lengths.shape[0]
        width = target.shape[1]
        fits = (
            dp == 2**4
            and mp > 1
            and chan % (2 * LANES) == 0
            and tok % LANES == 0
            and frames % CHUNK == 0
            and width % (dp // 4 * LANES) == 0
            and width % (dp * 8) == 0
            and kernel.shape[0] % 2 == 1
            and kernel.shape[0] <= 31
        )
        return fast_body(dp, mp, *args) if fits else plain_body(*args)

    return jax.shard_map(
        body,
        mesh=mesh,
        in_specs=(
            P("dp", "mp"),
            P("dp"),
            P("mp"),
            P("mp"),
            P(None, "mp"),
            P("dp", "mp"),
            P("dp", None),
        ),
        out_specs=(P("dp", "mp"), P("dp", "mp"), P(None, "mp"), P("mp"), P("mp")),
        check_vma=False,
    )
```

```python
import functools

import jax
import jax.numpy as jnp
from jax import lax
from jax.experimental import pallas as pl
from jax.experimental.pallas import tpu as pltpu
from jax.sharding import PartitionSpec as P

epsilon = 1e-05
LANES = 128
CHUNK = 64
F32 = jnp.float32
BF16 = jnp.bfloat16


def depthwise(inputs, taps):
    half = (taps.shape[0] - 1) // 2
    return lax.conv_general_dilated(
        inputs,
        taps[:, None, :],
        (1,),
        [(half, half)],
        dimension_numbers=("NWC", "WIO", "NWC"),
        feature_group_count=inputs.shape[2],
        precision=lax.Precision.HIGHEST,
    )


def plain_body(frames_in, lengths, ln_gain, ln_bias, kernel, point_weight, target):
    tok_rows, chan_count = frames_in.shape
    utt_count = lengths.shape[0]
    frame_count = tok_rows // utt_count
    full_width = target.shape[1]
    position = lax.broadcasted_iota(jnp.int32, (utt_count, frame_count), 1)
    valid_mask = (position < lengths[:, None]).astype(jnp.float32).reshape(tok_rows, 1)
    local_total = jnp.sum(lengths).astype(jnp.float32)
    values = frames_in.astype(jnp.float32)
    row_mean = lax.psum(jnp.sum(values, axis=1), "mp") / full_width
    centered = values - row_mean[:, None]
    row_var = lax.psum(jnp.sum(centered * centered, axis=1), "mp") / full_width
    inv_std = lax.rsqrt(row_var + epsilon)[:, None]
    normed = centered * inv_std
    masked = (normed * ln_gain + ln_bias) * valid_mask
    conv_out, conv_back = jax.vjp(
        depthwise, masked.reshape(utt_count, frame_count, chan_count), kernel
    )
    pre_act = conv_out.reshape(tok_rows, chan_count)
    gate_sig = jax.nn.sigmoid(pre_act)
    activation = (pre_act * gate_sig).astype(jnp.bfloat16)
    cotangent = target * valid_mask.astype(jnp.bfloat16)
    act_grad = jnp.dot(
        cotangent,
        lax.all_gather(point_weight, "dp", axis=0, tiled=True),
        preferred_element_type=jnp.float32,
    )
    pre_grad = act_grad * gate_sig * (1.0 + pre_act * (1.0 - gate_sig))
    back_in, kernel_part = conv_back(pre_grad.reshape(utt_count, frame_count, chan_count))
    masked_grad = back_in.reshape(tok_rows, chan_count) * valid_mask
    gain_part = jnp.sum(masked_grad * normed, axis=0)
    bias_part = jnp.sum(masked_grad, axis=0)
    hat_grad = masked_grad * ln_gain
    hat_sum, hat_dot = lax.psum(
        (jnp.sum(hat_grad, axis=1), jnp.sum(hat_grad * normed, axis=1)), "mp"
    )
    norm_grad = inv_std * (
        hat_grad - hat_sum[:, None] / full_width - normed * (hat_dot[:, None] / full_width)
    )
    term = lax.dot_general(
        cotangent, activation, (((0,), (0,)), ((), ())), preferred_element_type=jnp.float32
    )
    weight_grad = lax.psum_scatter(term, "dp", scatter_dimension=0, tiled=True)
    kernel_sum, gain_sum, bias_sum, frame_total = lax.psum(
        (kernel_part, gain_part, bias_part, local_total), "dp"
    )
    inverse = 1.0 / frame_total
    own_grad = lax.dynamic_slice_in_dim(
        cotangent, lax.axis_index("mp") * chan_count, chan_count, 1
    ).astype(jnp.float32)
    slot_total = tok_rows * lax.axis_size("dp")
    frames_grad = ((own_grad + norm_grad) * (slot_total * inverse)).astype(jnp.bfloat16)
    return (
        frames_grad,
        weight_grad * inverse,
        kernel_sum * inverse,
        gain_sum * inverse,
        bias_sum * inverse,
    )


def rcopy(src, dst, sends, recvs, at, peer):
    return pltpu.make_async_remote_copy(
        src_ref=src,
        dst_ref=dst,
        send_sem=sends.at[at],
        recv_sem=recvs.at[at],
        device_id=peer,
        device_id_type=pl.DeviceIdType.MESH,
    )


def mp_peers(mp):
    me_dp, me_mp = lax.axis_index("dp"), lax.axis_index("mp")
    return [(me_dp, lax.rem(me_mp + s, mp)) for s in range(1, mp)]


def dp_bits(stages):
    me_dp, me_mp = lax.axis_index("dp"), lax.axis_index("mp")
    bits = [(me_dp // (1 << s)) % 2 for s in range(stages)]
    peers = [(me_dp + (1 << s) * (1 - 2 * bits[s]), me_mp) for s in range(stages)]
    return bits, peers


def greet(peers):
    barrier = pltpu.get_barrier_semaphore()
    for peer in peers:
        pl.semaphore_signal(
            barrier, inc=1, device_id=peer, device_id_type=pl.DeviceIdType.MESH
        )
    pl.semaphore_wait(barrier, len(peers))


def eye_mask():
    shape = (LANES, LANES)
    return lax.broadcasted_iota(jnp.int32, shape, 0) == lax.broadcasted_iota(jnp.int32, shape, 1)


def to_row(column, eye):
    return jnp.sum(jnp.where(eye, column, 0.0), axis=0, keepdims=True)


def to_column(row, eye):
    return jnp.sum(jnp.where(eye, row, 0.0), axis=1, keepdims=True)


def lane_at(c):
    return pl.ds(pl.multiple_of(c * LANES, LANES), LANES)


def rows_at(start, size, unit):
    return pl.ds(pl.multiple_of(start, unit), size)


def valid_rows(len_ref, u, start, size):
    position = start + lax.broadcasted_iota(jnp.int32, (size, LANES), 0)
    return position < len_ref[u]


def fused_kernel(
    mp, stages, utts, frames, taps, pad,
    len_ref, x_ref, gain_ref, bias_ref, tap_ref, own_weight_ref, target_ref,
    out_ref, wgrad_ref, taps_ref, gain_out, bias_out,
    masked_ref, pre_ref, act_ref, cot_ref, mean_ref, rstd_ref, weight_ref,
    term, core_got, a1, a2, a3, b1, b2, b3,
    pgrad, hat, hat_sum, hat_dot, tap_acc, stat, got, hat_stat, hat_got,
    count, count_got, small, small_got,
    stat_s, stat_r, all_s, all_r,
    core_s, core_r, ring_s, ring_r, hat_s, hat_r, cnt_s, cnt_r, sm_s, sm_r, fetch_sem,
):
    tok, chan = x_ref.shape
    groups = tok // LANES
    blocks = chan // LANES
    span = frames + 2 * pad
    width = cot_ref.shape[1]
    per_utt = frames // CHUNK
    half = chan // 2
    out_rows = wgrad_ref.shape[0]
    highs = term.shape[0]
    row_peers = mp_peers(mp)
    bits, peers = dp_bits(stages)
    fetch = pltpu.make_async_copy(target_ref, cot_ref, fetch_sem)
    fetch.start()
    greet(peers + row_peers)
    core, why, zlo, zhi = bits
    eye = eye_mask()
    weight_ref[zhi, zlo, why, core] = own_weight_ref[...]
    pieces = [
        weight_ref.at[zhi, zlo, why, core],
        weight_ref.at[:, zlo, why, core],
        weight_ref.at[:, :, why, core],
        weight_ref.at[:, :, :, core],
    ]
    gathers = [
        rcopy(piece, piece, all_s, all_r, i, peers[stages - 1 - i])
        for i, piece in enumerate(pieces)
    ]
    gathers[0].start()

    def stats(g, _):
        values = x_ref[rows_at(g * LANES, LANES, LANES), :].astype(F32)
        local = jnp.sum(values, axis=1, keepdims=True) * (1.0 / chan)
        off = values - local
        squares = jnp.sum(off * off, axis=1, keepdims=True)
        stat[0, pl.ds(g, 1), :] = to_row(local, eye)
        stat[1, pl.ds(g, 1), :] = to_row(squares, eye)
        return 0

    lax.fori_loop(0, groups, stats, 0)
    copies = [
        rcopy(stat, got.at[s], stat_s, stat_r, s, peer) for s, peer in enumerate(row_peers)
    ]
    for copy in copies:
        copy.start()

    def mask_target(i, _):
        u, part = i // (frames // CHUNK), i % (frames // CHUNK)
        rows = rows_at(i * CHUNK, CHUNK, CHUNK)
        valid = valid_rows(len_ref, u, part * CHUNK, CHUNK)
        for c in range(width // LANES):
            lanes = pl.ds(c * LANES, LANES)
            block = cot_ref[rows, lanes].astype(F32)
            cot_ref[rows, lanes] = jnp.where(valid, block, 0.0).astype(BF16)
        return 0

    fetch.wait()
    lax.fori_loop(0, tok // CHUNK, mask_target, 0)

    def clear(i, _):
        c, u = i // utts, i % utts
        edge = jnp.zeros((pad, LANES), F32)
        masked_ref[c, rows_at(u * span, pad, pad), :] = edge
        masked_ref[c, rows_at(u * span + pad + frames, pad, pad), :] = edge
        pgrad[c, rows_at(u * span, pad, pad), :] = edge
        pgrad[c, rows_at(u * span + pad + frames, pad, pad), :] = edge
        return 0

    lax.fori_loop(0, blocks * utts, clear, 0)
    for copy in copies:
        copy.wait()
    mean = stat[0]
    for s in range(mp - 1):
        mean = mean + got[s, 0]
    mean = mean * (1.0 / mp)
    squares = stat[1] + chan * (stat[0] - mean) * (stat[0] - mean)
    for s in range(mp - 1):
        squares = squares + (got[s, 1] + chan * (got[s, 0] - mean) * (got[s, 0] - mean))
    stat[0] = mean
    stat[1] = lax.rsqrt(squares * (1.0 / (chan * mp)) + epsilon)

    gathers[0].wait()
    gathers[1].start()

    def spread_norm(g, _):
        rows = rows_at(g * LANES, LANES, LANES)
        shape = (LANES, LANES)
        mean_ref[rows, :] = jnp.broadcast_to(to_column(stat[0, pl.ds(g, 1), :], eye), shape)
        rstd_ref[rows, :] = jnp.broadcast_to(to_column(stat[1, pl.ds(g, 1), :], eye), shape)
        return 0

    lax.fori_loop(0, groups, spread_norm, 0)

    def forward_block(c, _):
        lanes = lane_at(c)
        gain, bias = gain_ref[:, lanes], bias_ref[:, lanes]

        def norm(i, _):
            u, part = i // (frames // CHUNK), i % (frames // CHUNK)
            rows = rows_at(i * CHUNK, CHUNK, CHUNK)
            values = x_ref[rows, lanes].astype(F32)
            normed = (values - mean_ref[rows, :]) * rstd_ref[rows, :]
            valid = valid_rows(len_ref, u, part * CHUNK, CHUNK)
            masked_ref[c, rows_at(u * span + pad + part * CHUNK, CHUNK, 16), :] = jnp.where(
                valid, normed * gain + bias, 0.0
            )
            return 0

        lax.fori_loop(0, tok // CHUNK, norm, 0)

        def conv(i, _):
            u, part = i // (frames // CHUNK), i % (frames // CHUNK)
            rows = rows_at(i * CHUNK, CHUNK, CHUNK)
            base = u * span + part * CHUNK
            shift = pad - (taps - 1) // 2
            total = jnp.zeros((CHUNK, LANES), F32)
            for b in range(8):
                ks = [k for k in range(taps) if (k + shift) % 8 == b]
                reach = 8 * max((k + shift) // 8 for k in ks)
                slab = masked_ref[c, pl.ds(base + b, CHUNK + reach), :]
                for k in ks:
                    at = (k + shift) // 8 * 8
                    total = total + tap_ref[pl.ds(k, 1), lanes] * slab[at:at + CHUNK]
            pre_ref[c, rows, :] = total
            act_ref[rows, lanes] = (total * jax.nn.sigmoid(total)).astype(BF16)
            return 0

        lax.fori_loop(0, tok // CHUNK, conv, 0)
        return 0

    lax.fori_loop(0, blocks // 3, forward_block, 0)
    gathers[1].wait()
    gathers[2].start()
    lax.fori_loop(blocks // 3, blocks, forward_block, 0)

    total = len_ref[0]
    for u in range(1, utts):
        total = total + len_ref[u]
    count[0] = jnp.full((8, LANES), total, jnp.int32).astype(F32)
    cnt = [
        rcopy(count.at[s], count_got.at[s], cnt_s, cnt_r, s, peers[s]) for s in range(stages)
    ]
    cnt[0].start()
    core_copies = []
    group_rows = width // highs
    for g in range(highs):
        if g == highs - 1:
            gathers[2].wait()
            gathers[3].start()
        product = lax.dot_general(
            cot_ref[:, g * group_rows:(g + 1) * group_rows],
            act_ref[...],
            (((0,), (0,)), ((), ())),
            preferred_element_type=F32,
        )
        for y in range(2):
            for k in range(2):
                at = (2 * y + k) * out_rows
                term[g, y, k] = product[at:at + out_rows]
        copy = rcopy(
            term.at[g, :, 1 - core], core_got.at[g], core_s, core_r, g, peers[0]
        )
        copy.start()
        core_copies.append(copy)
        cnt[g].wait()
        count[g + 1] = count[g] + count_got[g]
        if g + 1 < stages:
            cnt[g + 1].start()
    inverse = 1.0 / count[stages]

    for copy in core_copies:
        copy.wait()

    def join_core(i, _):
        g, y = i // 2, i % 2
        core_got[g, y] = core_got[g, y] + term[g, y, core]
        return 0

    lax.fori_loop(0, highs * 2, join_core, 0)
    left, right = pl.ds(0, half), pl.ds(half, half)

    copy_a1 = rcopy(core_got.at[:, 1 - why, :, left], a1, ring_s, ring_r, 0, peers[1])
    copies_b1 = [
        rcopy(
            core_got.at[2 * h + 1 - zlo, :, :, right], b1.at[h], ring_s, ring_r, 1 + h, peers[2]
        )
        for h in range(2)
    ]
    copies_a2 = [
        rcopy(a1.at[2 * h + 1 - zlo], a2.at[h], ring_s, ring_r, 3 + h, peers[2])
        for h in range(2)
    ]
    copy_b2 = rcopy(b1.at[1 - zhi], b2, ring_s, ring_r, 5, peers[3])
    copy_a3 = rcopy(a2.at[1 - zhi], a3, ring_s, ring_r, 6, peers[3])
    copy_b3 = rcopy(b2.at[1 - why], b3, ring_s, ring_r, 7, peers[1])

    copy_a1.start()
    for copy in copies_b1:
        copy.start()

    def act_grad(u, _):
        rows = rows_at(u * frames, frames, frames)
        product = jnp.dot(
            cot_ref[rows, :], weight_ref[...].reshape(width, chan), preferred_element_type=F32
        )
        for c in range(blocks):
            pre = pre_ref[c, rows, :]
            gate = jax.nn.sigmoid(pre)
            grad = product[:, c * LANES:(c + 1) * LANES]
            pgrad[c, rows_at(u * span + pad, frames, 16), :] = (
                grad * gate * (1.0 + pre * (1.0 - gate))
            )
        return 0

    gathers[3].wait()
    lax.fori_loop(0, utts, act_grad, 0)

    def second_stage():
        copy_a1.wait()
        for h in range(highs):
            a1[h] = a1[h] + core_got[h, why, :, left]
        for copy in copies_a2:
            copy.start()
        for copy in copies_b1:
            copy.wait()
        for h in range(2):
            for y in range(2):
                b1[h, y] = b1[h, y] + core_got[2 * h + zlo, y, :, right]
        copy_b2.start()

    def third_stage():
        for copy in copies_a2:
            copy.wait()
        for h in range(2):
            a2[h] = a2[h] + a1[2 * h + zlo]
        copy_a3.start()
        copy_b2.wait()
        for y in range(2):
            b2[y] = b2[y] + b1[zhi, y]
        copy_b3.start()

    def last_stage():
        scale = inverse[0:1, 0:1]
        copy_a3.wait()
        wgrad_ref[:, 0:half] = (a3[...] + a2[zhi]) * scale
        copy_b3.wait()
        wgrad_ref[:, half:chan] = (b3[...] + b2[why]) * scale

    shift = pad - (taps - 1) // 2

    def block(c, _):
        lanes = lane_at(c)
        gain = gain_ref[:, lanes]
        tap_acc[...] = jnp.zeros_like(tap_acc)

        def part_of(i, _):
            u, part = i // per_utt, i % per_utt
            rows = rows_at(i * CHUNK, CHUNK, CHUNK)
            base = u * span + part * CHUNK
            total = jnp.zeros((CHUNK, LANES), F32)
            grads = pgrad[c, rows_at(base + pad, CHUNK, 16), :]
            for b in range(8):
                ks = [k for k in range(taps) if (k + shift) % 8 == b]
                reach = 8 * max((k + shift) // 8 for k in ks)
                slab = pgrad[c, pl.ds(base + b, CHUNK + reach), :]
                for k in ks:
                    at = (k + shift) // 8 * 8
                    total = total + tap_ref[pl.ds(taps - 1 - k, 1), lanes] * slab[at:at + CHUNK]
            for b in range(8):
                ks = [k for k in range(taps) if (k + shift) % 8 == b]
                reach = 8 * max((k + shift) // 8 for k in ks)
                slab = masked_ref[c, pl.ds(base + b, CHUNK + reach), :]
                for k in ks:
                    at = (k + shift) // 8 * 8
                    part_sum = grads * slab[at:at + CHUNK]
                    tap_acc[k] += jnp.sum(part_sum.reshape(CHUNK // 8, 8, LANES), axis=0)
            valid = valid_rows(len_ref, u, part * CHUNK, CHUNK)
            masked_grad = jnp.where(valid, total, 0.0)
            normed = (x_ref[rows, lanes].astype(F32) - mean_ref[rows, :]) * rstd_ref[rows, :]
            scaled = masked_grad * normed
            tap_acc[taps] += jnp.sum(scaled.reshape(CHUNK // 8, 8, LANES), axis=0)
            tap_acc[taps + 1] += jnp.sum(masked_grad.reshape(CHUNK // 8, 8, LANES), axis=0)
            grad = masked_grad * gain
            hat[c, rows, :] = grad
            hat_sum[rows, :] += grad
            hat_dot[rows, :] += scaled * gain
            return 0

        lax.fori_loop(0, tok // CHUNK, part_of, 0)
        sums = jnp.sum(tap_acc[...], axis=1)
        small[c // (blocks // 2), 0, :, lane_at(c % (blocks // 2))] = sums
        return 0

    def reset(i, _):
        rows = rows_at(i * CHUNK, CHUNK, CHUNK)
        hat_sum[rows, :] = jnp.zeros((CHUNK, LANES), F32)
        hat_dot[rows, :] = jnp.zeros((CHUNK, LANES), F32)
        return 0

    lax.fori_loop(0, tok // CHUNK, reset, 0)
    sm = [
        [
            rcopy(
                small.at[p, s], small_got.at[p, s], sm_s, sm_r, p * stages + s, peers[s]
            )
            for s in range(stages)
        ]
        for p in range(2)
    ]

    def advance(p, s):
        sm[p][s].wait()
        small[p, s + 1] = small[p, s] + small_got[p, s]
        if s + 1 < stages:
            sm[p][s + 1].start()

    lax.fori_loop(0, blocks // 2, block, 0)
    second_stage()
    sm[0][0].start()
    left_over = blocks - blocks // 2
    for s in range(3):
        lax.fori_loop(
            blocks // 2 + left_over * s // 3, blocks // 2 + left_over * (s + 1) // 3, block, 0
        )
        if s < 2:
            advance(0, s)
    sm[1][0].start()
    advance(0, 2)

    def collect(g, _):
        rows = rows_at(g * LANES, LANES, LANES)
        hat_stat[0, pl.ds(g, 1), :] = to_row(jnp.sum(hat_sum[rows, :], axis=1, keepdims=True), eye)
        hat_stat[1, pl.ds(g, 1), :] = to_row(jnp.sum(hat_dot[rows, :], axis=1, keepdims=True), eye)
        return 0

    lax.fori_loop(0, groups, collect, 0)
    hats = [
        rcopy(hat_stat, hat_got.at[s], hat_s, hat_r, s, peer) for s, peer in enumerate(row_peers)
    ]
    for copy in hats:
        copy.start()
    advance(1, 0)
    for copy in hats:
        copy.wait()
    for j in range(2):
        joined = hat_stat[j]
        for s in range(mp - 1):
            joined = joined + hat_got[s, j]
        hat_stat[j] = joined * (1.0 / width)

    def spread(g, _):
        rows = rows_at(g * LANES, LANES, LANES)
        shape = (LANES, LANES)
        hat_sum[rows, :] = jnp.broadcast_to(to_column(hat_stat[0, pl.ds(g, 1), :], eye), shape)
        hat_dot[rows, :] = jnp.broadcast_to(to_column(hat_stat[1, pl.ds(g, 1), :], eye), shape)
        return 0

    lax.fori_loop(0, groups, spread, 0)
    own = lax.axis_index("mp") * blocks
    slots = (tok * (1 << stages)) * inverse[0:1, :]

    def finish(i, _):
        rows = rows_at(i * CHUNK, CHUNK, CHUNK)
        mean, rstd = mean_ref[rows, :], rstd_ref[rows, :]
        sums, dots = hat_sum[rows, :], hat_dot[rows, :]
        for c in range(blocks):
            lanes = pl.ds(c * LANES, LANES)
            normed = (x_ref[rows, lanes].astype(F32) - mean) * rstd
            grad = rstd * (hat[c, rows, :] - sums - normed * dots)
            direct = cot_ref[rows, lane_at(own + c)].astype(F32)
            out_ref[rows, lanes] = ((direct + grad) * slots).astype(BF16)
        return 0

    parts = tok // CHUNK
    lax.fori_loop(0, parts // 3, finish, 0)
    advance(1, 1)
    third_stage()
    lax.fori_loop(parts // 3, parts * 2 // 3, finish, 0)
    advance(0, 3)
    advance(1, 2)
    lax.fori_loop(parts * 2 // 3, parts, finish, 0)
    advance(1, 3)
    for p, part in enumerate((left, right)):
        sums = small[p, stages] * inverse[0:1, 0:1]
        taps_ref[:, part] = sums[:taps]
        gain_out[part] = sums[taps]
        bias_out[part] = sums[taps + 1]
    last_stage()


def fast_body(dp, mp, frames_in, lengths, ln_gain, ln_bias, kernel, point_weight, target):
    tok, chan = frames_in.shape
    utts = lengths.shape[0]
    frames = tok // utts
    width = target.shape[1]
    taps = kernel.shape[0]
    pad = 16
    blocks = chan // LANES
    stages = dp.bit_length() - 1
    groups = tok // LANES
    span = utts * (frames + 2 * pad)
    out_rows = width // dp
    highs = dp // 4
    half = chan // 2
    gain = ln_gain.reshape(1, chan)
    bias = ln_bias.reshape(1, chan)
    vmem = pl.BlockSpec(memory_space=pltpu.VMEM)
    smem = pl.BlockSpec(memory_space=pltpu.SMEM)
    dma = pltpu.SemaphoreType.DMA
    shape = jax.ShapeDtypeStruct
    peers = max(mp - 1, 1)
    side = (taps + 2 + 7) // 8 * 8
    return pl.pallas_call(
        functools.partial(fused_kernel, mp, stages, utts, frames, taps, pad),
        out_shape=(
            shape((tok, chan), BF16),
            shape((out_rows, chan), F32),
            shape((taps, chan), F32),
            shape((chan,), F32),
            shape((chan,), F32),
        ),
        in_specs=[smem] + [vmem] * 5 + [pl.BlockSpec(memory_space=pl.ANY)],
        out_specs=(vmem,) * 5,
        scratch_shapes=[
            pltpu.VMEM((blocks, span, LANES), F32),
            pltpu.VMEM((blocks, tok, LANES), F32),
            pltpu.VMEM((tok, chan), BF16),
            pltpu.VMEM((tok, width), BF16),
            pltpu.VMEM((tok, LANES), F32),
            pltpu.VMEM((tok, LANES), F32),
            pltpu.VMEM((2, 2, 2, 2, out_rows, chan), BF16),
            pltpu.VMEM((highs, 2, 2, out_rows, chan), F32),
            pltpu.VMEM((highs, 2, out_rows, chan), F32),
            pltpu.VMEM((highs, out_rows, half), F32),
            pltpu.VMEM((2, out_rows, half), F32),
            pltpu.VMEM((out_rows, half), F32),
            pltpu.VMEM((2, 2, out_rows, half), F32),
            pltpu.VMEM((2, out_rows, half), F32),
            pltpu.VMEM((out_rows, half), F32),
            pltpu.VMEM((blocks, span, LANES), F32),
            pltpu.VMEM((blocks, tok, LANES), F32),
            pltpu.VMEM((tok, LANES), F32),
            pltpu.VMEM((tok, LANES), F32),
            pltpu.VMEM((side, 8, LANES), F32),
            pltpu.VMEM((2, groups, LANES), F32),
            pltpu.VMEM((peers, 2, groups, LANES), F32),
            pltpu.VMEM((2, groups, LANES), F32),
            pltpu.VMEM((peers, 2, groups, LANES), F32),
            pltpu.VMEM((stages + 1, 8, LANES), F32),
            pltpu.VMEM((stages, 8, LANES), F32),
            pltpu.VMEM((2, stages + 1, side, half), F32),
            pltpu.VMEM((2, stages, side, half), F32),
            dma((peers,)),
            dma((peers,)),
            dma((stages,)),
            dma((stages,)),
            dma((highs,)),
            dma((highs,)),
            dma((8,)),
            dma((8,)),
            dma((peers,)),
            dma((peers,)),
            dma((stages,)),
            dma((stages,)),
            dma((2 * stages,)),
            dma((2 * stages,)),
            dma(()),
        ],
        compiler_params=pltpu.CompilerParams(
            collective_id=0, has_side_effects=True, vmem_limit_bytes=56 * 2**20
        ),
        name="fused",
    )(lengths, frames_in, gain, bias, kernel, point_weight, target)


def solution(mesh):
    dp, mp = mesh.shape["dp"], mesh.shape["mp"]

    def body(frames_in, lengths, ln_gain, ln_bias, kernel, point_weight, target):
        args = (frames_in, lengths, ln_gain, ln_bias, kernel, point_weight, target)
        tok, chan = frames_in.shape
        frames = tok // lengths.shape[0]
        width = target.shape[1]
        fits = (
            dp == 2**4
            and mp > 1
            and chan % (2 * LANES) == 0
            and tok % LANES == 0
            and frames % CHUNK == 0
            and width % (dp // 4 * LANES) == 0
            and width % (dp * 16) == 0
            and kernel.shape[0] % 2 == 1
            and kernel.shape[0] <= 31
        )
        return fast_body(dp, mp, *args) if fits else plain_body(*args)

    return jax.shard_map(
        body,
        mesh=mesh,
        in_specs=(
            P("dp", "mp"),
            P("dp"),
            P("mp"),
            P("mp"),
            P(None, "mp"),
            P("dp", "mp"),
            P("dp", None),
        ),
        out_specs=(P("dp", "mp"), P("dp", "mp"), P(None, "mp"), P("mp"), P("mp")),
        check_vma=False,
    )
```

```python
import functools

import jax
import jax.numpy as jnp
from jax import lax
from jax.experimental import pallas as pl
from jax.experimental.pallas import tpu as pltpu
from jax.sharding import PartitionSpec as P

epsilon = 1e-05
LANES = 128
CHUNK = 64
F32 = jnp.float32
BF16 = jnp.bfloat16


def depthwise(inputs, taps):
    half = (taps.shape[0] - 1) // 2
    return lax.conv_general_dilated(
        inputs,
        taps[:, None, :],
        (1,),
        [(half, half)],
        dimension_numbers=("NWC", "WIO", "NWC"),
        feature_group_count=inputs.shape[2],
        precision=lax.Precision.HIGHEST,
    )


def plain_body(frames_in, lengths, ln_gain, ln_bias, kernel, point_weight, target):
    tok_rows, chan_count = frames_in.shape
    utt_count = lengths.shape[0]
    frame_count = tok_rows // utt_count
    full_width = target.shape[1]
    position = lax.broadcasted_iota(jnp.int32, (utt_count, frame_count), 1)
    valid_mask = (position < lengths[:, None]).astype(jnp.float32).reshape(tok_rows, 1)
    local_total = jnp.sum(lengths).astype(jnp.float32)
    values = frames_in.astype(jnp.float32)
    row_mean = lax.psum(jnp.sum(values, axis=1), "mp") / full_width
    centered = values - row_mean[:, None]
    row_var = lax.psum(jnp.sum(centered * centered, axis=1), "mp") / full_width
    inv_std = lax.rsqrt(row_var + epsilon)[:, None]
    normed = centered * inv_std
    masked = (normed * ln_gain + ln_bias) * valid_mask
    conv_out, conv_back = jax.vjp(
        depthwise, masked.reshape(utt_count, frame_count, chan_count), kernel
    )
    pre_act = conv_out.reshape(tok_rows, chan_count)
    gate_sig = jax.nn.sigmoid(pre_act)
    activation = (pre_act * gate_sig).astype(jnp.bfloat16)
    cotangent = target * valid_mask.astype(jnp.bfloat16)
    act_grad = jnp.dot(
        cotangent,
        lax.all_gather(point_weight, "dp", axis=0, tiled=True),
        preferred_element_type=jnp.float32,
    )
    pre_grad = act_grad * gate_sig * (1.0 + pre_act * (1.0 - gate_sig))
    back_in, kernel_part = conv_back(pre_grad.reshape(utt_count, frame_count, chan_count))
    masked_grad = back_in.reshape(tok_rows, chan_count) * valid_mask
    gain_part = jnp.sum(masked_grad * normed, axis=0)
    bias_part = jnp.sum(masked_grad, axis=0)
    hat_grad = masked_grad * ln_gain
    hat_sum, hat_dot = lax.psum(
        (jnp.sum(hat_grad, axis=1), jnp.sum(hat_grad * normed, axis=1)), "mp"
    )
    norm_grad = inv_std * (
        hat_grad - hat_sum[:, None] / full_width - normed * (hat_dot[:, None] / full_width)
    )
    term = lax.dot_general(
        cotangent, activation, (((0,), (0,)), ((), ())), preferred_element_type=jnp.float32
    )
    weight_grad = lax.psum_scatter(term, "dp", scatter_dimension=0, tiled=True)
    kernel_sum, gain_sum, bias_sum, frame_total = lax.psum(
        (kernel_part, gain_part, bias_part, local_total), "dp"
    )
    inverse = 1.0 / frame_total
    own_grad = lax.dynamic_slice_in_dim(
        cotangent, lax.axis_index("mp") * chan_count, chan_count, 1
    ).astype(jnp.float32)
    slot_total = tok_rows * lax.axis_size("dp")
    frames_grad = ((own_grad + norm_grad) * (slot_total * inverse)).astype(jnp.bfloat16)
    return (
        frames_grad,
        weight_grad * inverse,
        kernel_sum * inverse,
        gain_sum * inverse,
        bias_sum * inverse,
    )


def rcopy(src, dst, sends, recvs, at, peer):
    return pltpu.make_async_remote_copy(
        src_ref=src,
        dst_ref=dst,
        send_sem=sends.at[at],
        recv_sem=recvs.at[at],
        device_id=peer,
        device_id_type=pl.DeviceIdType.MESH,
    )


def mp_peers(mp):
    me_dp, me_mp = lax.axis_index("dp"), lax.axis_index("mp")
    return [(me_dp, lax.rem(me_mp + s, mp)) for s in range(1, mp)]


def dp_bits(stages):
    me_dp, me_mp = lax.axis_index("dp"), lax.axis_index("mp")
    bits = [(me_dp // (1 << s)) % 2 for s in range(stages)]
    peers = [(me_dp + (1 << s) * (1 - 2 * bits[s]), me_mp) for s in range(stages)]
    return bits, peers


def greet(peers):
    barrier = pltpu.get_barrier_semaphore()
    for peer in peers:
        pl.semaphore_signal(
            barrier, inc=1, device_id=peer, device_id_type=pl.DeviceIdType.MESH
        )
    pl.semaphore_wait(barrier, len(peers))


def eye_mask():
    shape = (LANES, LANES)
    return lax.broadcasted_iota(jnp.int32, shape, 0) == lax.broadcasted_iota(jnp.int32, shape, 1)


def to_row(column, eye):
    return jnp.sum(jnp.where(eye, column, 0.0), axis=0, keepdims=True)


def to_column(row, eye):
    return jnp.sum(jnp.where(eye, row, 0.0), axis=1, keepdims=True)


def lane_at(c):
    return pl.ds(pl.multiple_of(c * LANES, LANES), LANES)


def rows_at(start, size, unit):
    return pl.ds(pl.multiple_of(start, unit), size)


def valid_rows(len_ref, u, start, size):
    position = start + lax.broadcasted_iota(jnp.int32, (size, LANES), 0)
    return position < len_ref[u]


def fused_kernel(
    mp, stages, utts, frames, taps, pad,
    len_ref, x_ref, gain_ref, bias_ref, tap_ref, own_weight_ref, target_ref,
    out_ref, wgrad_ref, taps_ref, gain_out, bias_out,
    masked_ref, pre_ref, act_ref, cot_ref, mean_ref, rstd_ref, weight_ref,
    term, core_got, a1, a2, a3, b1, b2, b3,
    pgrad, hat, hat_sum, hat_dot, tap_acc, stat, got, hat_stat, hat_got,
    count, count_got, small, small_got,
    stat_s, stat_r, all_s, all_r,
    core_s, core_r, ring_s, ring_r, hat_s, hat_r, cnt_s, cnt_r, sm_s, sm_r, fetch_sem,
):
    tok, chan = x_ref.shape
    groups = tok // LANES
    blocks = chan // LANES
    span = frames + 2 * pad
    width = cot_ref.shape[1]
    per_utt = frames // CHUNK
    half = chan // 2
    out_rows = wgrad_ref.shape[0]
    highs = term.shape[0]
    row_peers = mp_peers(mp)
    bits, peers = dp_bits(stages)
    fetch = pltpu.make_async_copy(target_ref, cot_ref, fetch_sem)
    fetch.start()
    greet(peers + row_peers)
    core, why, zlo, zhi = bits
    eye = eye_mask()
    left, right = pl.ds(0, half), pl.ds(half, half)
    weight_ref[zhi, zlo, why, core] = own_weight_ref[...]
    gather_a = [
        (weight_ref.at[zhi, zlo, why, core, :, left], 3),
        (weight_ref.at[:, zlo, why, core, :, left], 2),
        (weight_ref.at[:, :, why, core, :, left], 1),
        (weight_ref.at[:, :, :, core, :, left], 0),
    ]
    gather_b = [
        (weight_ref.at[zhi, zlo, why, core, :, right], 1),
        (weight_ref.at[zhi, zlo, :, core, :, right], 3),
        (weight_ref.at[:, zlo, :, core, :, right], 2),
        (weight_ref.at[:, :, :, core, :, right], 0),
    ]
    gathers = [
        [
            rcopy(piece, piece, all_s, all_r, p * stages + i, peers[bit])
            for i, (piece, bit) in enumerate(pieces)
        ]
        for p, pieces in enumerate((gather_a, gather_b))
    ]

    def gather_next(p, i):
        gathers[p][i].wait()
        gathers[p][i + 1].start()

    gathers[0][0].start()
    gathers[1][0].start()
    total = len_ref[0]
    for u in range(1, utts):
        total = total + len_ref[u]
    count[0] = jnp.full((8, LANES), total, jnp.int32).astype(F32)
    cnt = [
        rcopy(count.at[s], count_got.at[s], cnt_s, cnt_r, s, peers[s]) for s in range(stages)
    ]
    cnt[0].start()

    def count_next(s):
        cnt[s].wait()
        count[s + 1] = count[s] + count_got[s]
        if s + 1 < stages:
            cnt[s + 1].start()

    def stats(g, _):
        values = x_ref[rows_at(g * LANES, LANES, LANES), :].astype(F32)
        local = jnp.sum(values, axis=1, keepdims=True) * (1.0 / chan)
        off = values - local
        squares = jnp.sum(off * off, axis=1, keepdims=True)
        stat[0, pl.ds(g, 1), :] = to_row(local, eye)
        stat[1, pl.ds(g, 1), :] = to_row(squares, eye)
        return 0

    lax.fori_loop(0, groups, stats, 0)
    copies = [
        rcopy(stat, got.at[s], stat_s, stat_r, s, peer) for s, peer in enumerate(row_peers)
    ]
    for copy in copies:
        copy.start()

    def mask_target(i, _):
        u, part = i // (frames // CHUNK), i % (frames // CHUNK)
        rows = rows_at(i * CHUNK, CHUNK, CHUNK)
        valid = valid_rows(len_ref, u, part * CHUNK, CHUNK)
        for c in range(width // LANES):
            lanes = pl.ds(c * LANES, LANES)
            block = cot_ref[rows, lanes].astype(F32)
            cot_ref[rows, lanes] = jnp.where(valid, block, 0.0).astype(BF16)
        return 0

    fetch.wait()
    lax.fori_loop(0, tok // CHUNK, mask_target, 0)

    def clear(i, _):
        c, u = i // utts, i % utts
        edge = jnp.zeros((pad, LANES), F32)
        masked_ref[c, rows_at(u * span, pad, pad), :] = edge
        masked_ref[c, rows_at(u * span + pad + frames, pad, pad), :] = edge
        pgrad[c, rows_at(u * span, pad, pad), :] = edge
        pgrad[c, rows_at(u * span + pad + frames, pad, pad), :] = edge
        return 0

    lax.fori_loop(0, blocks * utts, clear, 0)
    for copy in copies:
        copy.wait()
    mean = stat[0]
    for s in range(mp - 1):
        mean = mean + got[s, 0]
    mean = mean * (1.0 / mp)
    squares = stat[1] + chan * (stat[0] - mean) * (stat[0] - mean)
    for s in range(mp - 1):
        squares = squares + (got[s, 1] + chan * (got[s, 0] - mean) * (got[s, 0] - mean))
    stat[0] = mean
    stat[1] = lax.rsqrt(squares * (1.0 / (chan * mp)) + epsilon)

    gather_next(0, 0)
    gather_next(1, 0)

    def spread_norm(g, _):
        rows = rows_at(g * LANES, LANES, LANES)
        shape = (LANES, LANES)
        mean_ref[rows, :] = jnp.broadcast_to(to_column(stat[0, pl.ds(g, 1), :], eye), shape)
        rstd_ref[rows, :] = jnp.broadcast_to(to_column(stat[1, pl.ds(g, 1), :], eye), shape)
        return 0

    lax.fori_loop(0, groups, spread_norm, 0)

    def forward_block(c, _):
        lanes = lane_at(c)
        gain, bias = gain_ref[:, lanes], bias_ref[:, lanes]

        def norm(i, _):
            u, part = i // (frames // CHUNK), i % (frames // CHUNK)
            rows = rows_at(i * CHUNK, CHUNK, CHUNK)
            values = x_ref[rows, lanes].astype(F32)
            normed = (values - mean_ref[rows, :]) * rstd_ref[rows, :]
            valid = valid_rows(len_ref, u, part * CHUNK, CHUNK)
            masked_ref[c, rows_at(u * span + pad + part * CHUNK, CHUNK, 16), :] = jnp.where(
                valid, normed * gain + bias, 0.0
            )
            return 0

        lax.fori_loop(0, tok // CHUNK, norm, 0)

        def conv(i, _):
            u, part = i // (frames // CHUNK), i % (frames // CHUNK)
            rows = rows_at(i * CHUNK, CHUNK, CHUNK)
            base = u * span + part * CHUNK
            shift = pad - (taps - 1) // 2
            total = jnp.zeros((CHUNK, LANES), F32)
            for b in range(8):
                ks = [k for k in range(taps) if (k + shift) % 8 == b]
                reach = 8 * max((k + shift) // 8 for k in ks)
                slab = masked_ref[c, pl.ds(base + b, CHUNK + reach), :]
                for k in ks:
                    at = (k + shift) // 8 * 8
                    total = total + tap_ref[pl.ds(k, 1), lanes] * slab[at:at + CHUNK]
            pre_ref[c, rows, :] = total
            act_ref[rows, lanes] = (total * jax.nn.sigmoid(total)).astype(BF16)
            return 0

        lax.fori_loop(0, tok // CHUNK, conv, 0)
        return 0

    for s in range(6):
        lax.fori_loop(blocks * s // 6, blocks * (s + 1) // 6, forward_block, 0)
        if s < stages:
            count_next(s)
        if s == 1:
            gather_next(0, 1)
            gather_next(1, 1)
        if s == 4:
            gather_next(0, 2)
            gather_next(1, 2)

    core_copies = []
    group_rows = width // highs
    for g in range(highs):
        product = lax.dot_general(
            cot_ref[:, g * group_rows:(g + 1) * group_rows],
            act_ref[...],
            (((0,), (0,)), ((), ())),
            preferred_element_type=F32,
        )
        for y in range(2):
            for k in range(2):
                at = (2 * y + k) * out_rows
                term[g, y, k] = product[at:at + out_rows]
        copy = rcopy(
            term.at[g, :, 1 - core], core_got.at[g], core_s, core_r, g, peers[0]
        )
        copy.start()
        core_copies.append(copy)
    inverse = 1.0 / count[stages]

    for copy in core_copies:
        copy.wait()

    def join_core(i, _):
        g, y = i // 2, i % 2
        core_got[g, y] = core_got[g, y] + term[g, y, core]
        return 0

    lax.fori_loop(0, highs * 2, join_core, 0)

    copy_a1 = rcopy(core_got.at[:, 1 - why, :, left], a1, ring_s, ring_r, 0, peers[1])
    copies_b1 = [
        rcopy(
            core_got.at[2 * h + 1 - zlo, :, :, right], b1.at[h], ring_s, ring_r, 1 + h, peers[2]
        )
        for h in range(2)
    ]
    copies_a2 = [
        rcopy(a1.at[2 * h + 1 - zlo], a2.at[h], ring_s, ring_r, 3 + h, peers[2])
        for h in range(2)
    ]
    copy_b2 = rcopy(b1.at[1 - zhi], b2, ring_s, ring_r, 5, peers[3])
    copy_a3 = rcopy(a2.at[1 - zhi], a3, ring_s, ring_r, 6, peers[3])
    copy_b3 = rcopy(b2.at[1 - why], b3, ring_s, ring_r, 7, peers[1])

    copy_a1.start()
    for copy in copies_b1:
        copy.start()

    def act_grad(u, _):
        rows = rows_at(u * frames, frames, frames)
        product = jnp.dot(
            cot_ref[rows, :], weight_ref[...].reshape(width, chan), preferred_element_type=F32
        )
        for c in range(blocks):
            pre = pre_ref[c, rows, :]
            gate = jax.nn.sigmoid(pre)
            grad = product[:, c * LANES:(c + 1) * LANES]
            pgrad[c, rows_at(u * span + pad, frames, 16), :] = (
                grad * gate * (1.0 + pre * (1.0 - gate))
            )
        return 0

    gathers[0][3].wait()
    gathers[1][3].wait()
    lax.fori_loop(0, utts, act_grad, 0)

    def second_stage():
        copy_a1.wait()
        for h in range(highs):
            a1[h] = a1[h] + core_got[h, why, :, left]
        for copy in copies_a2:
            copy.start()
        for copy in copies_b1:
            copy.wait()
        for h in range(2):
            for y in range(2):
                b1[h, y] = b1[h, y] + core_got[2 * h + zlo, y, :, right]
        copy_b2.start()

    def third_stage():
        for copy in copies_a2:
            copy.wait()
        for h in range(2):
            a2[h] = a2[h] + a1[2 * h + zlo]
        copy_a3.start()
        copy_b2.wait()
        for y in range(2):
            b2[y] = b2[y] + b1[zhi, y]
        copy_b3.start()

    def last_stage():
        scale = inverse[0:1, 0:1]
        copy_a3.wait()
        wgrad_ref[:, 0:half] = (a3[...] + a2[zhi]) * scale
        copy_b3.wait()
        wgrad_ref[:, half:chan] = (b3[...] + b2[why]) * scale

    shift = pad - (taps - 1) // 2

    def block(c, _):
        lanes = lane_at(c)
        gain = gain_ref[:, lanes]
        tap_acc[...] = jnp.zeros_like(tap_acc)

        def part_of(i, _):
            u, part = i // per_utt, i % per_utt
            rows = rows_at(i * CHUNK, CHUNK, CHUNK)
            base = u * span + part * CHUNK
            total = jnp.zeros((CHUNK, LANES), F32)
            grads = pgrad[c, rows_at(base + pad, CHUNK, 16), :]
            for b in range(8):
                ks = [k for k in range(taps) if (k + shift) % 8 == b]
                reach = 8 * max((k + shift) // 8 for k in ks)
                slab = pgrad[c, pl.ds(base + b, CHUNK + reach), :]
                for k in ks:
                    at = (k + shift) // 8 * 8
                    total = total + tap_ref[pl.ds(taps - 1 - k, 1), lanes] * slab[at:at + CHUNK]
            for b in range(8):
                ks = [k for k in range(taps) if (k + shift) % 8 == b]
                reach = 8 * max((k + shift) // 8 for k in ks)
                slab = masked_ref[c, pl.ds(base + b, CHUNK + reach), :]
                for k in ks:
                    at = (k + shift) // 8 * 8
                    part_sum = grads * slab[at:at + CHUNK]
                    tap_acc[k] += jnp.sum(part_sum.reshape(CHUNK // 8, 8, LANES), axis=0)
            valid = valid_rows(len_ref, u, part * CHUNK, CHUNK)
            masked_grad = jnp.where(valid, total, 0.0)
            normed = (x_ref[rows, lanes].astype(F32) - mean_ref[rows, :]) * rstd_ref[rows, :]
            scaled = masked_grad * normed
            tap_acc[taps] += jnp.sum(scaled.reshape(CHUNK // 8, 8, LANES), axis=0)
            tap_acc[taps + 1] += jnp.sum(masked_grad.reshape(CHUNK // 8, 8, LANES), axis=0)
            grad = masked_grad * gain
            hat[c, rows, :] = grad
            hat_sum[rows, :] += grad
            hat_dot[rows, :] += scaled * gain
            return 0

        lax.fori_loop(0, tok // CHUNK, part_of, 0)
        sums = jnp.sum(tap_acc[...], axis=1)
        small[c // (blocks // 2), 0, :, lane_at(c % (blocks // 2))] = sums
        return 0

    def reset(i, _):
        rows = rows_at(i * CHUNK, CHUNK, CHUNK)
        hat_sum[rows, :] = jnp.zeros((CHUNK, LANES), F32)
        hat_dot[rows, :] = jnp.zeros((CHUNK, LANES), F32)
        return 0

    lax.fori_loop(0, tok // CHUNK, reset, 0)
    sm = [
        [
            rcopy(
                small.at[p, s], small_got.at[p, s], sm_s, sm_r, p * stages + s, peers[s]
            )
            for s in range(stages)
        ]
        for p in range(2)
    ]

    def advance(p, s):
        sm[p][s].wait()
        small[p, s + 1] = small[p, s] + small_got[p, s]
        if s + 1 < stages:
            sm[p][s + 1].start()

    lax.fori_loop(0, blocks // 2, block, 0)
    second_stage()
    sm[0][0].start()
    left_over = blocks - blocks // 2
    for s in range(3):
        lax.fori_loop(
            blocks // 2 + left_over * s // 3, blocks // 2 + left_over * (s + 1) // 3, block, 0
        )
        if s < 2:
            advance(0, s)
    sm[1][0].start()
    advance(0, 2)

    def collect(g, _):
        rows = rows_at(g * LANES, LANES, LANES)
        hat_stat[0, pl.ds(g, 1), :] = to_row(jnp.sum(hat_sum[rows, :], axis=1, keepdims=True), eye)
        hat_stat[1, pl.ds(g, 1), :] = to_row(jnp.sum(hat_dot[rows, :], axis=1, keepdims=True), eye)
        return 0

    lax.fori_loop(0, groups, collect, 0)
    hats = [
        rcopy(hat_stat, hat_got.at[s], hat_s, hat_r, s, peer) for s, peer in enumerate(row_peers)
    ]
    for copy in hats:
        copy.start()
    advance(1, 0)
    for copy in hats:
        copy.wait()
    third_stage()
    for j in range(2):
        joined = hat_stat[j]
        for s in range(mp - 1):
            joined = joined + hat_got[s, j]
        hat_stat[j] = joined * (1.0 / width)

    def spread(g, _):
        rows = rows_at(g * LANES, LANES, LANES)
        shape = (LANES, LANES)
        hat_sum[rows, :] = jnp.broadcast_to(to_column(hat_stat[0, pl.ds(g, 1), :], eye), shape)
        hat_dot[rows, :] = jnp.broadcast_to(to_column(hat_stat[1, pl.ds(g, 1), :], eye), shape)
        return 0

    lax.fori_loop(0, groups, spread, 0)
    own = lax.axis_index("mp") * blocks
    slots = (tok * (1 << stages)) * inverse[0:1, :]

    def finish(i, _):
        rows = rows_at(i * CHUNK, CHUNK, CHUNK)
        mean, rstd = mean_ref[rows, :], rstd_ref[rows, :]
        sums, dots = hat_sum[rows, :], hat_dot[rows, :]
        for c in range(blocks):
            lanes = pl.ds(c * LANES, LANES)
            normed = (x_ref[rows, lanes].astype(F32) - mean) * rstd
            grad = rstd * (hat[c, rows, :] - sums - normed * dots)
            direct = cot_ref[rows, lane_at(own + c)].astype(F32)
            out_ref[rows, lanes] = ((direct + grad) * slots).astype(BF16)
        return 0

    parts = tok // CHUNK
    lax.fori_loop(0, parts // 3, finish, 0)
    advance(1, 1)
    lax.fori_loop(parts // 3, parts * 2 // 3, finish, 0)
    advance(0, 3)
    advance(1, 2)
    lax.fori_loop(parts * 2 // 3, parts, finish, 0)
    advance(1, 3)
    for p, part in enumerate((left, right)):
        sums = small[p, stages] * inverse[0:1, 0:1]
        taps_ref[:, part] = sums[:taps]
        gain_out[part] = sums[taps]
        bias_out[part] = sums[taps + 1]
    last_stage()


def fast_body(dp, mp, frames_in, lengths, ln_gain, ln_bias, kernel, point_weight, target):
    tok, chan = frames_in.shape
    utts = lengths.shape[0]
    frames = tok // utts
    width = target.shape[1]
    taps = kernel.shape[0]
    pad = 16
    blocks = chan // LANES
    stages = dp.bit_length() - 1
    groups = tok // LANES
    span = utts * (frames + 2 * pad)
    out_rows = width // dp
    highs = dp // 4
    half = chan // 2
    gain = ln_gain.reshape(1, chan)
    bias = ln_bias.reshape(1, chan)
    vmem = pl.BlockSpec(memory_space=pltpu.VMEM)
    smem = pl.BlockSpec(memory_space=pltpu.SMEM)
    dma = pltpu.SemaphoreType.DMA
    shape = jax.ShapeDtypeStruct
    peers = max(mp - 1, 1)
    side = (taps + 2 + 7) // 8 * 8
    return pl.pallas_call(
        functools.partial(fused_kernel, mp, stages, utts, frames, taps, pad),
        out_shape=(
            shape((tok, chan), BF16),
            shape((out_rows, chan), F32),
            shape((taps, chan), F32),
            shape((chan,), F32),
            shape((chan,), F32),
        ),
        in_specs=[smem] + [vmem] * 5 + [pl.BlockSpec(memory_space=pl.ANY)],
        out_specs=(vmem,) * 5,
        scratch_shapes=[
            pltpu.VMEM((blocks, span, LANES), F32),
            pltpu.VMEM((blocks, tok, LANES), F32),
            pltpu.VMEM((tok, chan), BF16),
            pltpu.VMEM((tok, width), BF16),
            pltpu.VMEM((tok, LANES), F32),
            pltpu.VMEM((tok, LANES), F32),
            pltpu.VMEM((2, 2, 2, 2, out_rows, chan), BF16),
            pltpu.VMEM((highs, 2, 2, out_rows, chan), F32),
            pltpu.VMEM((highs, 2, out_rows, chan), F32),
            pltpu.VMEM((highs, out_rows, half), F32),
            pltpu.VMEM((2, out_rows, half), F32),
            pltpu.VMEM((out_rows, half), F32),
            pltpu.VMEM((2, 2, out_rows, half), F32),
            pltpu.VMEM((2, out_rows, half), F32),
            pltpu.VMEM((out_rows, half), F32),
            pltpu.VMEM((blocks, span, LANES), F32),
            pltpu.VMEM((blocks, tok, LANES), F32),
            pltpu.VMEM((tok, LANES), F32),
            pltpu.VMEM((tok, LANES), F32),
            pltpu.VMEM((side, 8, LANES), F32),
            pltpu.VMEM((2, groups, LANES), F32),
            pltpu.VMEM((peers, 2, groups, LANES), F32),
            pltpu.VMEM((2, groups, LANES), F32),
            pltpu.VMEM((peers, 2, groups, LANES), F32),
            pltpu.VMEM((stages + 1, 8, LANES), F32),
            pltpu.VMEM((stages, 8, LANES), F32),
            pltpu.VMEM((2, stages + 1, side, half), F32),
            pltpu.VMEM((2, stages, side, half), F32),
            dma((peers,)),
            dma((peers,)),
            dma((2 * stages,)),
            dma((2 * stages,)),
            dma((highs,)),
            dma((highs,)),
            dma((8,)),
            dma((8,)),
            dma((peers,)),
            dma((peers,)),
            dma((stages,)),
            dma((stages,)),
            dma((2 * stages,)),
            dma((2 * stages,)),
            dma(()),
        ],
        compiler_params=pltpu.CompilerParams(
            collective_id=0, has_side_effects=True, vmem_limit_bytes=56 * 2**20
        ),
        name="fused",
    )(lengths, frames_in, gain, bias, kernel, point_weight, target)


def solution(mesh):
    dp, mp = mesh.shape["dp"], mesh.shape["mp"]

    def body(frames_in, lengths, ln_gain, ln_bias, kernel, point_weight, target):
        args = (frames_in, lengths, ln_gain, ln_bias, kernel, point_weight, target)
        tok, chan = frames_in.shape
        frames = tok // lengths.shape[0]
        width = target.shape[1]
        fits = (
            dp == 2**4
            and mp > 1
            and chan % (2 * LANES) == 0
            and tok % LANES == 0
            and frames % CHUNK == 0
            and width % (dp // 4 * LANES) == 0
            and width % (dp * 16) == 0
            and kernel.shape[0] % 2 == 1
            and kernel.shape[0] <= 31
        )
        return fast_body(dp, mp, *args) if fits else plain_body(*args)

    return jax.shard_map(
        body,
        mesh=mesh,
        in_specs=(
            P("dp", "mp"),
            P("dp"),
            P("mp"),
            P("mp"),
            P(None, "mp"),
            P("dp", "mp"),
            P("dp", None),
        ),
        out_specs=(P("dp", "mp"), P("dp", "mp"), P(None, "mp"), P("mp"), P("mp")),
        check_vma=False,
    )
```

```python
import functools

import jax
import jax.numpy as jnp
from jax import lax
from jax.experimental import pallas as pl
from jax.experimental.pallas import tpu as pltpu
from jax.sharding import PartitionSpec as P

epsilon = 1e-05
LANES = 128
CHUNK = 64
F32 = jnp.float32
BF16 = jnp.bfloat16


def depthwise(inputs, taps):
    half = (taps.shape[0] - 1) // 2
    return lax.conv_general_dilated(
        inputs,
        taps[:, None, :],
        (1,),
        [(half, half)],
        dimension_numbers=("NWC", "WIO", "NWC"),
        feature_group_count=inputs.shape[2],
        precision=lax.Precision.HIGHEST,
    )


def plain_body(frames_in, lengths, ln_gain, ln_bias, kernel, point_weight, target):
    tok_rows, chan_count = frames_in.shape
    utt_count = lengths.shape[0]
    frame_count = tok_rows // utt_count
    full_width = target.shape[1]
    position = lax.broadcasted_iota(jnp.int32, (utt_count, frame_count), 1)
    valid_mask = (position < lengths[:, None]).astype(jnp.float32).reshape(tok_rows, 1)
    local_total = jnp.sum(lengths).astype(jnp.float32)
    values = frames_in.astype(jnp.float32)
    row_mean = lax.psum(jnp.sum(values, axis=1), "mp") / full_width
    centered = values - row_mean[:, None]
    row_var = lax.psum(jnp.sum(centered * centered, axis=1), "mp") / full_width
    inv_std = lax.rsqrt(row_var + epsilon)[:, None]
    normed = centered * inv_std
    masked = (normed * ln_gain + ln_bias) * valid_mask
    conv_out, conv_back = jax.vjp(
        depthwise, masked.reshape(utt_count, frame_count, chan_count), kernel
    )
    pre_act = conv_out.reshape(tok_rows, chan_count)
    gate_sig = jax.nn.sigmoid(pre_act)
    activation = (pre_act * gate_sig).astype(jnp.bfloat16)
    cotangent = target * valid_mask.astype(jnp.bfloat16)
    act_grad = jnp.dot(
        cotangent,
        lax.all_gather(point_weight, "dp", axis=0, tiled=True),
        preferred_element_type=jnp.float32,
    )
    pre_grad = act_grad * gate_sig * (1.0 + pre_act * (1.0 - gate_sig))
    back_in, kernel_part = conv_back(pre_grad.reshape(utt_count, frame_count, chan_count))
    masked_grad = back_in.reshape(tok_rows, chan_count) * valid_mask
    gain_part = jnp.sum(masked_grad * normed, axis=0)
    bias_part = jnp.sum(masked_grad, axis=0)
    hat_grad = masked_grad * ln_gain
    hat_sum, hat_dot = lax.psum(
        (jnp.sum(hat_grad, axis=1), jnp.sum(hat_grad * normed, axis=1)), "mp"
    )
    norm_grad = inv_std * (
        hat_grad - hat_sum[:, None] / full_width - normed * (hat_dot[:, None] / full_width)
    )
    term = lax.dot_general(
        cotangent, activation, (((0,), (0,)), ((), ())), preferred_element_type=jnp.float32
    )
    weight_grad = lax.psum_scatter(term, "dp", scatter_dimension=0, tiled=True)
    kernel_sum, gain_sum, bias_sum, frame_total = lax.psum(
        (kernel_part, gain_part, bias_part, local_total), "dp"
    )
    inverse = 1.0 / frame_total
    own_grad = lax.dynamic_slice_in_dim(
        cotangent, lax.axis_index("mp") * chan_count, chan_count, 1
    ).astype(jnp.float32)
    slot_total = tok_rows * lax.axis_size("dp")
    frames_grad = ((own_grad + norm_grad) * (slot_total * inverse)).astype(jnp.bfloat16)
    return (
        frames_grad,
        weight_grad * inverse,
        kernel_sum * inverse,
        gain_sum * inverse,
        bias_sum * inverse,
    )


def rcopy(src, dst, sends, recvs, at, peer):
    return pltpu.make_async_remote_copy(
        src_ref=src,
        dst_ref=dst,
        send_sem=sends.at[at],
        recv_sem=recvs.at[at],
        device_id=peer,
        device_id_type=pl.DeviceIdType.MESH,
    )


def mp_peers(mp):
    me_dp, me_mp = lax.axis_index("dp"), lax.axis_index("mp")
    return [(me_dp, lax.rem(me_mp + s, mp)) for s in range(1, mp)]


def dp_bits(stages):
    me_dp, me_mp = lax.axis_index("dp"), lax.axis_index("mp")
    bits = [(me_dp // (1 << s)) % 2 for s in range(stages)]
    peers = [(me_dp + (1 << s) * (1 - 2 * bits[s]), me_mp) for s in range(stages)]
    return bits, peers


def greet(peers):
    barrier = pltpu.get_barrier_semaphore()
    for peer in peers:
        pl.semaphore_signal(
            barrier, inc=1, device_id=peer, device_id_type=pl.DeviceIdType.MESH
        )
    pl.semaphore_wait(barrier, len(peers))


def eye_mask():
    shape = (LANES, LANES)
    return lax.broadcasted_iota(jnp.int32, shape, 0) == lax.broadcasted_iota(jnp.int32, shape, 1)


def to_row(column, eye):
    return jnp.sum(jnp.where(eye, column, 0.0), axis=0, keepdims=True)


def to_column(row, eye):
    return jnp.sum(jnp.where(eye, row, 0.0), axis=1, keepdims=True)


def lane_at(c):
    return pl.ds(pl.multiple_of(c * LANES, LANES), LANES)


def rows_at(start, size, unit):
    return pl.ds(pl.multiple_of(start, unit), size)


def valid_rows(len_ref, u, start, size):
    position = start + lax.broadcasted_iota(jnp.int32, (size, LANES), 0)
    return position < len_ref[u]


def fused_kernel(
    mp, stages, utts, frames, taps, pad,
    len_ref, x_ref, gain_in, bias_in, tap_ref, own_weight_ref, target_ref,
    out_ref, wgrad_ref, taps_ref, gain_out, bias_out,
    gain_ref, bias_ref, masked_ref, pre_ref, act_ref, cot_ref, mean_ref, rstd_ref, weight_ref,
    term, core_got, a1, a2, a3, b1, b2, b3,
    pgrad, hat, hat_sum, hat_dot, tap_acc, stat, got, hat_stat, hat_got,
    count, count_got, small, small_got,
    stat_s, stat_r, all_s, all_r,
    core_s, core_r, ring_s, ring_r, hat_s, hat_r, cnt_s, cnt_r, sm_s, sm_r, fetch_sem,
):
    tok, chan = x_ref.shape
    groups = tok // LANES
    blocks = chan // LANES
    span = frames + 2 * pad
    width = cot_ref.shape[1]
    per_utt = frames // CHUNK
    half = chan // 2
    out_rows = wgrad_ref.shape[0]
    highs = term.shape[0]
    row_peers = mp_peers(mp)
    bits, peers = dp_bits(stages)
    fetch = pltpu.make_async_copy(target_ref, cot_ref, fetch_sem)
    fetch.start()
    gain_ref[...] = gain_in[...].reshape(1, chan)
    bias_ref[...] = bias_in[...].reshape(1, chan)
    greet(peers + row_peers)
    core, why, zlo, zhi = bits
    eye = eye_mask()
    left, right = pl.ds(0, half), pl.ds(half, half)
    weight_ref[zhi, zlo, why, core] = own_weight_ref[...]
    gather_a = [
        (weight_ref.at[zhi, zlo, why, core, :, left], 3),
        (weight_ref.at[:, zlo, why, core, :, left], 2),
        (weight_ref.at[:, :, why, core, :, left], 1),
        (weight_ref.at[:, :, :, core, :, left], 0),
    ]
    gather_b = [
        (weight_ref.at[zhi, zlo, why, core, :, right], 1),
        (weight_ref.at[zhi, zlo, :, core, :, right], 3),
        (weight_ref.at[:, zlo, :, core, :, right], 2),
        (weight_ref.at[:, :, :, core, :, right], 0),
    ]
    gathers = [
        [
            rcopy(piece, piece, all_s, all_r, p * stages + i, peers[bit])
            for i, (piece, bit) in enumerate(pieces)
        ]
        for p, pieces in enumerate((gather_a, gather_b))
    ]

    def gather_next(p, i):
        gathers[p][i].wait()
        gathers[p][i + 1].start()

    gathers[0][0].start()
    gathers[1][0].start()
    total = len_ref[0]
    for u in range(1, utts):
        total = total + len_ref[u]
    count[0] = jnp.full((8, LANES), total, jnp.int32).astype(F32)
    cnt = [
        rcopy(count.at[s], count_got.at[s], cnt_s, cnt_r, s, peers[s]) for s in range(stages)
    ]
    cnt[0].start()

    def count_next(s):
        cnt[s].wait()
        count[s + 1] = count[s] + count_got[s]
        if s + 1 < stages:
            cnt[s + 1].start()

    def stats(g, _):
        values = x_ref[rows_at(g * LANES, LANES, LANES), :].astype(F32)
        local = jnp.sum(values, axis=1, keepdims=True) * (1.0 / chan)
        off = values - local
        squares = jnp.sum(off * off, axis=1, keepdims=True)
        stat[0, pl.ds(g, 1), :] = to_row(local, eye)
        stat[1, pl.ds(g, 1), :] = to_row(squares, eye)
        return 0

    lax.fori_loop(0, groups, stats, 0)
    copies = [
        rcopy(stat, got.at[s], stat_s, stat_r, s, peer) for s, peer in enumerate(row_peers)
    ]
    for copy in copies:
        copy.start()

    def mask_target(i, _):
        u, part = i // (frames // CHUNK), i % (frames // CHUNK)
        rows = rows_at(i * CHUNK, CHUNK, CHUNK)
        valid = valid_rows(len_ref, u, part * CHUNK, CHUNK)
        for c in range(width // LANES):
            lanes = pl.ds(c * LANES, LANES)
            block = cot_ref[rows, lanes].astype(F32)
            cot_ref[rows, lanes] = jnp.where(valid, block, 0.0).astype(BF16)
        return 0

    fetch.wait()
    lax.fori_loop(0, tok // CHUNK, mask_target, 0)

    def clear(i, _):
        c, u = i // utts, i % utts
        edge = jnp.zeros((pad, LANES), F32)
        masked_ref[c, rows_at(u * span, pad, pad), :] = edge
        masked_ref[c, rows_at(u * span + pad + frames, pad, pad), :] = edge
        pgrad[c, rows_at(u * span, pad, pad), :] = edge
        pgrad[c, rows_at(u * span + pad + frames, pad, pad), :] = edge
        return 0

    lax.fori_loop(0, blocks * utts, clear, 0)
    for copy in copies:
        copy.wait()
    mean = stat[0]
    for s in range(mp - 1):
        mean = mean + got[s, 0]
    mean = mean * (1.0 / mp)
    squares = stat[1] + chan * (stat[0] - mean) * (stat[0] - mean)
    for s in range(mp - 1):
        squares = squares + (got[s, 1] + chan * (got[s, 0] - mean) * (got[s, 0] - mean))
    stat[0] = mean
    stat[1] = lax.rsqrt(squares * (1.0 / (chan * mp)) + epsilon)

    gather_next(0, 0)
    gather_next(1, 0)

    def spread_norm(g, _):
        rows = rows_at(g * LANES, LANES, LANES)
        shape = (LANES, LANES)
        mean_ref[rows, :] = jnp.broadcast_to(to_column(stat[0, pl.ds(g, 1), :], eye), shape)
        rstd_ref[rows, :] = jnp.broadcast_to(to_column(stat[1, pl.ds(g, 1), :], eye), shape)
        return 0

    lax.fori_loop(0, groups, spread_norm, 0)

    def forward_block(c, _):
        lanes = lane_at(c)
        gain, bias = gain_ref[:, lanes], bias_ref[:, lanes]

        def norm(i, _):
            u, part = i // (frames // CHUNK), i % (frames // CHUNK)
            rows = rows_at(i * CHUNK, CHUNK, CHUNK)
            values = x_ref[rows, lanes].astype(F32)
            normed = (values - mean_ref[rows, :]) * rstd_ref[rows, :]
            valid = valid_rows(len_ref, u, part * CHUNK, CHUNK)
            masked_ref[c, rows_at(u * span + pad + part * CHUNK, CHUNK, 16), :] = jnp.where(
                valid, normed * gain + bias, 0.0
            )
            return 0

        lax.fori_loop(0, tok // CHUNK, norm, 0)

        def conv(i, _):
            u, part = i // (frames // CHUNK), i % (frames // CHUNK)
            rows = rows_at(i * CHUNK, CHUNK, CHUNK)
            base = u * span + part * CHUNK
            shift = pad - (taps - 1) // 2
            total = jnp.zeros((CHUNK, LANES), F32)
            for b in range(8):
                ks = [k for k in range(taps) if (k + shift) % 8 == b]
                reach = 8 * max((k + shift) // 8 for k in ks)
                slab = masked_ref[c, pl.ds(base + b, CHUNK + reach), :]
                for k in ks:
                    at = (k + shift) // 8 * 8
                    total = total + tap_ref[pl.ds(k, 1), lanes] * slab[at:at + CHUNK]
            pre_ref[c, rows, :] = total
            act_ref[rows, lanes] = (total * jax.nn.sigmoid(total)).astype(BF16)
            return 0

        lax.fori_loop(0, tok // CHUNK, conv, 0)
        return 0

    for s in range(6):
        lax.fori_loop(blocks * s // 6, blocks * (s + 1) // 6, forward_block, 0)
        if s < stages:
            count_next(s)
        if s == 1:
            gather_next(0, 1)
            gather_next(1, 1)
        if s == 4:
            gather_next(0, 2)
            gather_next(1, 2)

    copies_a1 = [
        rcopy(core_got.at[g, 1 - why, :, left], a1.at[g], ring_s, ring_r, g, peers[1])
        for g in range(highs)
    ]
    copies_b1 = [
        rcopy(
            core_got.at[2 * h + 1 - zlo, :, :, right], b1.at[h], ring_s, ring_r, 4 + h, peers[2]
        )
        for h in range(2)
    ]
    copies_a2 = [
        rcopy(a1.at[2 * h + 1 - zlo], a2.at[h], ring_s, ring_r, 6 + h, peers[2])
        for h in range(2)
    ]
    copy_b2 = rcopy(b1.at[1 - zhi], b2, ring_s, ring_r, 8, peers[3])
    copy_a3 = rcopy(a2.at[1 - zhi], a3, ring_s, ring_r, 9, peers[3])
    copy_b3 = rcopy(b2.at[1 - why], b3, ring_s, ring_r, 10, peers[1])

    def join_core(g):
        core_copies[g].wait()
        for y in range(2):
            core_got[g, y] = core_got[g, y] + term[g, y, core]
        copies_a1[g].start()
        if g % 2 == 1:
            copies_b1[g // 2].start()

    core_copies = []
    group_rows = width // highs
    for g in range(highs):
        product = lax.dot_general(
            cot_ref[:, g * group_rows:(g + 1) * group_rows],
            act_ref[...],
            (((0,), (0,)), ((), ())),
            preferred_element_type=F32,
        )
        for y in range(2):
            for k in range(2):
                at = (2 * y + k) * out_rows
                term[g, y, k] = product[at:at + out_rows]
        copy = rcopy(
            term.at[g, :, 1 - core], core_got.at[g], core_s, core_r, g, peers[0]
        )
        copy.start()
        core_copies.append(copy)
        if g > 0:
            join_core(g - 1)
    inverse = 1.0 / count[stages]

    join_core(highs - 1)

    def act_grad(u, _):
        rows = rows_at(u * frames, frames, frames)
        product = jnp.dot(
            cot_ref[rows, :], weight_ref[...].reshape(width, chan), preferred_element_type=F32
        )
        for c in range(blocks):
            pre = pre_ref[c, rows, :]
            gate = jax.nn.sigmoid(pre)
            grad = product[:, c * LANES:(c + 1) * LANES]
            pgrad[c, rows_at(u * span + pad, frames, 16), :] = (
                grad * gate * (1.0 + pre * (1.0 - gate))
            )
        return 0

    gathers[0][3].wait()
    gathers[1][3].wait()
    lax.fori_loop(0, utts, act_grad, 0)

    def second_stage():
        for copy in copies_a1:
            copy.wait()
        for h in range(highs):
            a1[h] = a1[h] + core_got[h, why, :, left]
        for copy in copies_a2:
            copy.start()
        for copy in copies_b1:
            copy.wait()
        for h in range(2):
            for y in range(2):
                b1[h, y] = b1[h, y] + core_got[2 * h + zlo, y, :, right]
        copy_b2.start()

    def third_stage():
        for copy in copies_a2:
            copy.wait()
        for h in range(2):
            a2[h] = a2[h] + a1[2 * h + zlo]
        copy_a3.start()
        copy_b2.wait()
        for y in range(2):
            b2[y] = b2[y] + b1[zhi, y]
        copy_b3.start()

    def last_stage():
        scale = inverse[0:1, 0:1]
        copy_a3.wait()
        wgrad_ref[:, 0:half] = (a3[...] + a2[zhi]) * scale
        copy_b3.wait()
        wgrad_ref[:, half:chan] = (b3[...] + b2[why]) * scale

    shift = pad - (taps - 1) // 2

    def block(c, _):
        lanes = lane_at(c)
        gain = gain_ref[:, lanes]
        tap_acc[...] = jnp.zeros_like(tap_acc)

        def part_of(i, _):
            u, part = i // per_utt, i % per_utt
            rows = rows_at(i * CHUNK, CHUNK, CHUNK)
            base = u * span + part * CHUNK
            total = jnp.zeros((CHUNK, LANES), F32)
            grads = pgrad[c, rows_at(base + pad, CHUNK, 16), :]
            for b in range(8):
                ks = [k for k in range(taps) if (k + shift) % 8 == b]
                reach = 8 * max((k + shift) // 8 for k in ks)
                slab = pgrad[c, pl.ds(base + b, CHUNK + reach), :]
                for k in ks:
                    at = (k + shift) // 8 * 8
                    total = total + tap_ref[pl.ds(taps - 1 - k, 1), lanes] * slab[at:at + CHUNK]
            for b in range(8):
                ks = [k for k in range(taps) if (k + shift) % 8 == b]
                reach = 8 * max((k + shift) // 8 for k in ks)
                slab = masked_ref[c, pl.ds(base + b, CHUNK + reach), :]
                for k in ks:
                    at = (k + shift) // 8 * 8
                    part_sum = grads * slab[at:at + CHUNK]
                    tap_acc[k] += jnp.sum(part_sum.reshape(CHUNK // 8, 8, LANES), axis=0)
            valid = valid_rows(len_ref, u, part * CHUNK, CHUNK)
            masked_grad = jnp.where(valid, total, 0.0)
            normed = (x_ref[rows, lanes].astype(F32) - mean_ref[rows, :]) * rstd_ref[rows, :]
            scaled = masked_grad * normed
            tap_acc[taps] += jnp.sum(scaled.reshape(CHUNK // 8, 8, LANES), axis=0)
            tap_acc[taps + 1] += jnp.sum(masked_grad.reshape(CHUNK // 8, 8, LANES), axis=0)
            grad = masked_grad * gain
            hat[c, rows, :] = grad
            hat_sum[rows, :] += grad
            hat_dot[rows, :] += scaled * gain
            return 0

        lax.fori_loop(0, tok // CHUNK, part_of, 0)
        sums = jnp.sum(tap_acc[...], axis=1)
        small[c // (blocks // 2), 0, :, lane_at(c % (blocks // 2))] = sums
        return 0

    def reset(i, _):
        rows = rows_at(i * CHUNK, CHUNK, CHUNK)
        hat_sum[rows, :] = jnp.zeros((CHUNK, LANES), F32)
        hat_dot[rows, :] = jnp.zeros((CHUNK, LANES), F32)
        return 0

    lax.fori_loop(0, tok // CHUNK, reset, 0)
    sm = [
        [
            rcopy(
                small.at[p, s], small_got.at[p, s], sm_s, sm_r, p * stages + s, peers[s]
            )
            for s in range(stages)
        ]
        for p in range(2)
    ]

    def advance(p, s):
        sm[p][s].wait()
        small[p, s + 1] = small[p, s] + small_got[p, s]
        if s + 1 < stages:
            sm[p][s + 1].start()

    lax.fori_loop(0, blocks // 2, block, 0)
    second_stage()
    sm[0][0].start()
    left_over = blocks - blocks // 2
    for s in range(3):
        lax.fori_loop(
            blocks // 2 + left_over * s // 3, blocks // 2 + left_over * (s + 1) // 3, block, 0
        )
        if s < 2:
            advance(0, s)
    sm[1][0].start()
    advance(0, 2)

    def collect(g, _):
        rows = rows_at(g * LANES, LANES, LANES)
        hat_stat[0, pl.ds(g, 1), :] = to_row(jnp.sum(hat_sum[rows, :], axis=1, keepdims=True), eye)
        hat_stat[1, pl.ds(g, 1), :] = to_row(jnp.sum(hat_dot[rows, :], axis=1, keepdims=True), eye)
        return 0

    lax.fori_loop(0, groups, collect, 0)
    hats = [
        rcopy(hat_stat, hat_got.at[s], hat_s, hat_r, s, peer) for s, peer in enumerate(row_peers)
    ]
    for copy in hats:
        copy.start()
    advance(1, 0)
    for copy in hats:
        copy.wait()
    third_stage()
    for j in range(2):
        joined = hat_stat[j]
        for s in range(mp - 1):
            joined = joined + hat_got[s, j]
        hat_stat[j] = joined * (1.0 / width)

    def spread(g, _):
        rows = rows_at(g * LANES, LANES, LANES)
        shape = (LANES, LANES)
        hat_sum[rows, :] = jnp.broadcast_to(to_column(hat_stat[0, pl.ds(g, 1), :], eye), shape)
        hat_dot[rows, :] = jnp.broadcast_to(to_column(hat_stat[1, pl.ds(g, 1), :], eye), shape)
        return 0

    lax.fori_loop(0, groups, spread, 0)
    own = lax.axis_index("mp") * blocks
    slots = (tok * (1 << stages)) * inverse[0:1, :]

    def finish(i, _):
        rows = rows_at(i * CHUNK, CHUNK, CHUNK)
        mean, rstd = mean_ref[rows, :], rstd_ref[rows, :]
        sums, dots = hat_sum[rows, :], hat_dot[rows, :]
        for c in range(blocks):
            lanes = pl.ds(c * LANES, LANES)
            normed = (x_ref[rows, lanes].astype(F32) - mean) * rstd
            grad = rstd * (hat[c, rows, :] - sums - normed * dots)
            direct = cot_ref[rows, lane_at(own + c)].astype(F32)
            out_ref[rows, lanes] = ((direct + grad) * slots).astype(BF16)
        return 0

    parts = tok // CHUNK
    lax.fori_loop(0, parts // 3, finish, 0)
    advance(1, 1)
    lax.fori_loop(parts // 3, parts * 2 // 3, finish, 0)
    advance(0, 3)
    advance(1, 2)
    lax.fori_loop(parts * 2 // 3, parts, finish, 0)
    advance(1, 3)
    for p, part in enumerate((left, right)):
        sums = small[p, stages] * inverse[0:1, 0:1]
        taps_ref[:, part] = sums[:taps]
        gain_out[part] = sums[taps]
        bias_out[part] = sums[taps + 1]
    last_stage()


def fast_body(dp, mp, frames_in, lengths, ln_gain, ln_bias, kernel, point_weight, target):
    tok, chan = frames_in.shape
    utts = lengths.shape[0]
    frames = tok // utts
    width = target.shape[1]
    taps = kernel.shape[0]
    pad = 16
    blocks = chan // LANES
    stages = dp.bit_length() - 1
    groups = tok // LANES
    span = utts * (frames + 2 * pad)
    out_rows = width // dp
    highs = dp // 4
    half = chan // 2
    vmem = pl.BlockSpec(memory_space=pltpu.VMEM)
    smem = pl.BlockSpec(memory_space=pltpu.SMEM)
    dma = pltpu.SemaphoreType.DMA
    shape = jax.ShapeDtypeStruct
    peers = max(mp - 1, 1)
    side = (taps + 2 + 7) // 8 * 8
    return pl.pallas_call(
        functools.partial(fused_kernel, mp, stages, utts, frames, taps, pad),
        out_shape=(
            shape((tok, chan), BF16),
            shape((out_rows, chan), F32),
            shape((taps, chan), F32),
            shape((chan,), F32),
            shape((chan,), F32),
        ),
        in_specs=[smem] + [vmem] * 5 + [pl.BlockSpec(memory_space=pl.ANY)],
        out_specs=(vmem,) * 5,
        scratch_shapes=[
            pltpu.VMEM((1, chan), F32),
            pltpu.VMEM((1, chan), F32),
            pltpu.VMEM((blocks, span, LANES), F32),
            pltpu.VMEM((blocks, tok, LANES), F32),
            pltpu.VMEM((tok, chan), BF16),
            pltpu.VMEM((tok, width), BF16),
            pltpu.VMEM((tok, LANES), F32),
            pltpu.VMEM((tok, LANES), F32),
            pltpu.VMEM((2, 2, 2, 2, out_rows, chan), BF16),
            pltpu.VMEM((highs, 2, 2, out_rows, chan), F32),
            pltpu.VMEM((highs, 2, out_rows, chan), F32),
            pltpu.VMEM((highs, out_rows, half), F32),
            pltpu.VMEM((2, out_rows, half), F32),
            pltpu.VMEM((out_rows, half), F32),
            pltpu.VMEM((2, 2, out_rows, half), F32),
            pltpu.VMEM((2, out_rows, half), F32),
            pltpu.VMEM((out_rows, half), F32),
            pltpu.VMEM((blocks, span, LANES), F32),
            pltpu.VMEM((blocks, tok, LANES), F32),
            pltpu.VMEM((tok, LANES), F32),
            pltpu.VMEM((tok, LANES), F32),
            pltpu.VMEM((side, 8, LANES), F32),
            pltpu.VMEM((2, groups, LANES), F32),
            pltpu.VMEM((peers, 2, groups, LANES), F32),
            pltpu.VMEM((2, groups, LANES), F32),
            pltpu.VMEM((peers, 2, groups, LANES), F32),
            pltpu.VMEM((stages + 1, 8, LANES), F32),
            pltpu.VMEM((stages, 8, LANES), F32),
            pltpu.VMEM((2, stages + 1, side, half), F32),
            pltpu.VMEM((2, stages, side, half), F32),
            dma((peers,)),
            dma((peers,)),
            dma((2 * stages,)),
            dma((2 * stages,)),
            dma((highs,)),
            dma((highs,)),
            dma((11,)),
            dma((11,)),
            dma((peers,)),
            dma((peers,)),
            dma((stages,)),
            dma((stages,)),
            dma((2 * stages,)),
            dma((2 * stages,)),
            dma(()),
        ],
        compiler_params=pltpu.CompilerParams(
            collective_id=0, has_side_effects=True, vmem_limit_bytes=56 * 2**20
        ),
        name="fused",
    )(lengths, frames_in, ln_gain, ln_bias, kernel, point_weight, target)


def solution(mesh):
    dp, mp = mesh.shape["dp"], mesh.shape["mp"]

    def body(frames_in, lengths, ln_gain, ln_bias, kernel, point_weight, target):
        args = (frames_in, lengths, ln_gain, ln_bias, kernel, point_weight, target)
        tok, chan = frames_in.shape
        frames = tok // lengths.shape[0]
        width = target.shape[1]
        fits = (
            dp == 2**4
            and mp > 1
            and chan % (2 * LANES) == 0
            and tok % LANES == 0
            and frames % CHUNK == 0
            and width % (dp // 4 * LANES) == 0
            and width % (dp * 16) == 0
            and kernel.shape[0] % 2 == 1
            and kernel.shape[0] <= 31
        )
        return fast_body(dp, mp, *args) if fits else plain_body(*args)

    return jax.shard_map(
        body,
        mesh=mesh,
        in_specs=(
            P("dp", "mp"),
            P("dp"),
            P("mp"),
            P("mp"),
            P(None, "mp"),
            P("dp", "mp"),
            P("dp", None),
        ),
        out_specs=(P("dp", "mp"), P("dp", "mp"), P(None, "mp"), P("mp"), P("mp")),
        check_vma=False,
    )
```
